512 devices in a mesh: rows: 32 (over z, x), res: 16 (over y, core).
Axes of the slice: x: 4, y: 8, z: 8, core: 2. Of those that a mesh axis runs over, the one named last changes fastest.
Arguments:
- source_alignment_rows: bfloat16 [2048, 256, 256], P('rows', 'res'), may hold values from -120 to 120
- pairs: int32 [6, 2048], P(None, 'rows'), may hold values from -1 to 2047, as said below
- chain_first_residue: int32 [6], replicated, may hold values from 0 to 235, as said below
- gap_embedding: bfloat16 [256], replicated, may hold values from -4 to 4
- layer_norm_gain: bfloat16 [256], replicated, may hold values from 0.099609375 to 1.8984375
- layer_norm_bias: bfloat16 [256], replicated, may hold values from -3 to 3
- projection_weight: bfloat16 [256, 8, 128], replicated, may hold values from -0.375 to 0.375
- gate_bias_heads: bfloat16 [256], replicated, may hold values from -4 to 4
- pair_bias_logits: bfloat16 [8, 256, 256], P(None, 'res'), may hold values from -6 to 320
- output_weight: bfloat16 [256, 256], replicated, may hold values from -0.375 to 0.375
- output_bias: bfloat16 [256], replicated, may hold values from -3 to 3
Outputs:
- update: bfloat16 [2048, 256, 256], P('rows', 'res')
The draws below stay inside these ranges and needn't reach their ends.
Inputs may be any that keep to these rules, and one draw needn't show every extreme that they name: `pairs`: within one chain each source row is named at most once; chain 0 has no gaps. For each chain and each aligned block of 64 joint rows, at most 2 entries name rows of one aligned block of 64 source rows, and exactly 2 in some block. chain_first_residue[0] is 0, the starts rise, chain k holds residues from its start up to the next start (the last up to 256), and each chain has at least 21 residues; the last chain has exactly that many.
All inputs are finite; a program needn't handle non-finite values.
Results may differ from the reference program's by a relative error of at most 0.012.
Values may be sent and summed in bfloat16 or wider, within the bound.
A program may use at most 64 MiB of HBM per device.

```python
import math
import jax
import jax.numpy as jnp
from jax import lax

C_M = 256
HEADS = 8
HEAD_DIM = 32
CHAINS = 6
JOINT_DEV = 64
TOTAL_ROWS = 2048
RESIDUES = 256
CAP = 2


def draw_source_alignment_rows(key, part):
    key = jax.random.fold_in(key, 11)
    base_key, chan_key, cell_key = jax.random.split(key, 3)
    array_shape = (TOTAL_ROWS, RESIDUES, C_M)
    chan_scale = jnp.exp(jax.random.uniform(chan_key, (C_M,), jnp.float32, 0.0, math.log(10.0)))
    cell_scale = jnp.exp(jax.random.uniform(cell_key, (TOTAL_ROWS, RESIDUES, 1), jnp.float32, 0.0, math.log(3.0)))
    base = jnp.clip(jax.random.normal(base_key, array_shape, jnp.float32), -4.0, 4.0)
    return jnp.clip(base * chan_scale * cell_scale, -120.0, 120.0).astype(jnp.bfloat16)


def draw_pairs(key, part):
    key = jax.random.fold_in(key, 23)
    owners = TOTAL_ROWS // JOINT_DEV

    def chain_list(chain_index):
        chain_key = jax.random.fold_in(key, chain_index)
        offset_key, slot_key, place_key, gap_key = jax.random.split(chain_key, 4)
        offsets = jax.random.permutation(offset_key, owners)
        dest_ids = jnp.arange(owners, dtype=jnp.int32)
        source_dev = (dest_ids[:, None] + offsets[None, :]) % owners
        slot_scores = jax.random.randint(slot_key, (owners, owners, CAP), 0, 1 << 20) * CAP + jnp.arange(CAP, dtype=jnp.int32)
        slot_order = jnp.argsort(slot_scores, axis=-1).astype(jnp.int32)
        source_local = jnp.arange(owners, dtype=jnp.int32)[None, :, None] * CAP + slot_order
        flat_rows = (source_dev[:, :, None] * JOINT_DEV + source_local).reshape(owners, JOINT_DEV)
        place_scores = jax.random.randint(place_key, (owners, JOINT_DEV), 0, 1 << 20) * JOINT_DEV + jnp.arange(JOINT_DEV, dtype=jnp.int32)
        place_order = jnp.argsort(place_scores, axis=-1)
        placed = jnp.take_along_axis(flat_rows, place_order, axis=1)
        gap_draw = jax.random.randint(gap_key, (owners, JOINT_DEV), 0, 8)
        is_gap = (gap_draw < (dest_ids % 4)[:, None]) & (chain_index > 0)
        return jnp.where(is_gap, -1, placed).reshape(TOTAL_ROWS)
    return jnp.stack([chain_list(chain_index) for chain_index in range(CHAINS)]).astype(jnp.int32)


def draw_chain_first_residue(key, part):
    key = jax.random.fold_in(key, 37)
    least = RESIDUES // (2 * CHAINS)
    spare = RESIDUES - CHAINS * least
    cuts = jnp.sort(jax.random.randint(key, (CHAINS - 1,), 0, spare + 1))
    cuts = cuts.at[CHAINS - 2].set(spare)
    later = jnp.arange(1, CHAINS, dtype=jnp.int32) * least + cuts
    return jnp.concatenate([jnp.zeros((1,), jnp.int32), later.astype(jnp.int32)])


def draw_pair_bias_logits(key, part):
    key = jax.random.fold_in(key, 41)
    base_key = jax.random.fold_in(key, 0)
    array_shape = (HEADS, RESIDUES, RESIDUES)
    values = jnp.clip(1.5 * jax.random.normal(base_key, array_shape, jnp.float32), -6.0, 6.0)
    return values.astype(jnp.bfloat16)


def noise(rng, dims, width, reach, kind=jnp.bfloat16):
    return jnp.clip(width * jax.random.normal(rng, dims, jnp.float32), -reach, reach).astype(kind)


def setup_inputs(seed: int = 0) -> dict:
    keys = jax.random.split(jax.random.key(seed), 12)
    return {
        "source_alignment_rows": draw_source_alignment_rows(jax.random.fold_in(keys[11], 71), 0),
        "pairs": draw_pairs(jax.random.fold_in(keys[11], 71), 0),
        "chain_first_residue": draw_chain_first_residue(jax.random.fold_in(keys[11], 71), 0),
        "gap_embedding": noise(keys[3], (C_M,), 1.0, 4.0),
        "layer_norm_gain": jnp.clip(1.0 + 0.18 * jax.random.normal(keys[4], (C_M,), jnp.float32), 0.099609375, 1.8984375).astype(jnp.bfloat16),
        "layer_norm_bias": noise(keys[5], (C_M,), 0.5, 3.0),
        "projection_weight": noise(keys[6], (C_M, HEADS, 4 * HEAD_DIM), C_M ** -0.5, 0.375),
        "gate_bias_heads": noise(keys[7], (C_M,), 1.0, 4.0),
        "pair_bias_logits": draw_pair_bias_logits(jax.random.fold_in(keys[11], 71), 0),
        "output_weight": noise(keys[9], (C_M, C_M), C_M ** -0.5, 0.375),
        "output_bias": noise(keys[10], (C_M,), 0.5, 3.0),
    }


norm_eps = 1e-05
ref_block = 16

def layer_norm(values, gain, shift):
    widened = values.astype(jnp.float32)
    center = lax.optimization_barrier(jnp.mean(widened, axis=-1, keepdims=True))
    spread = lax.optimization_barrier(jnp.mean(jnp.square(widened - center), axis=-1, keepdims=True))
    scaled = (widened - center) * lax.rsqrt(spread + norm_eps)
    return (scaled * gain.astype(jnp.float32) + shift.astype(jnp.float32)).astype(jnp.bfloat16)

def reference(source_alignment_rows, pairs, chain_first_residue, gap_embedding, layer_norm_gain, layer_norm_bias, projection_weight, gate_bias_heads, pair_bias_logits, output_weight, output_bias):
    column_indices = jnp.arange(RESIDUES, dtype=jnp.int32)
    chain_of = lax.optimization_barrier(jnp.sum((column_indices[:, None] >= chain_first_residue[None, 1:]).astype(jnp.int32), axis=1)).astype(jnp.int32)
    column_lists = pairs[chain_of]
    proj_weight = projection_weight.astype(jnp.float32)
    out_weight = output_weight.astype(jnp.float32).reshape(HEADS, HEAD_DIM, C_M)
    bias_wide = pair_bias_logits.astype(jnp.float32)
    gate_shift = gate_bias_heads.astype(jnp.float32).reshape(HEADS, 1, HEAD_DIM)
    query_scale = HEAD_DIM ** (-0.5)

    def one_block(first_row):
        selected_rows = lax.dynamic_slice_in_dim(column_lists, first_row, ref_block, 1).T
        gathered_rows = source_alignment_rows[jnp.maximum(selected_rows, 0), column_indices[None, :]]
        joint_rows = jnp.where((selected_rows >= 0)[..., None], gathered_rows, gap_embedding[None, None, :])
        normed = layer_norm(joint_rows, layer_norm_gain, layer_norm_bias)
        projected = jnp.einsum('rcm,mhe->rhce', normed.astype(jnp.float32), proj_weight)
        queries = (projected[..., :HEAD_DIM] * query_scale).astype(jnp.bfloat16)
        key_rows = projected[..., HEAD_DIM:2 * HEAD_DIM].astype(jnp.bfloat16)
        value_rows = projected[..., 2 * HEAD_DIM:3 * HEAD_DIM].astype(jnp.bfloat16)
        gate_rows = jax.nn.sigmoid(projected[..., 3 * HEAD_DIM:] + gate_shift[None]).astype(jnp.bfloat16)
        scores = jnp.einsum('rhqd,rhkd->rhqk', queries.astype(jnp.float32), key_rows.astype(jnp.float32)) + bias_wide[None]
        highest = lax.optimization_barrier(jnp.max(scores, axis=-1, keepdims=True))
        lifted = jnp.exp(scores - highest)
        weights = (lifted / lax.optimization_barrier(jnp.sum(lifted, axis=-1, keepdims=True))).astype(jnp.bfloat16)
        summed = jnp.einsum('rhqk,rhkd->rhqd', weights.astype(jnp.float32), value_rows.astype(jnp.float32))
        attended = (summed * gate_rows.astype(jnp.float32)).astype(jnp.bfloat16)
        update = jnp.einsum('rhqd,hdm->rqm', attended.astype(jnp.float32), out_weight) + output_bias.astype(jnp.float32)
        return update.astype(jnp.bfloat16)
    firsts = jnp.arange(TOTAL_ROWS // ref_block, dtype=jnp.int32) * ref_block
    blocks = lax.map(one_block, firsts)
    return blocks.reshape(TOTAL_ROWS, RESIDUES, C_M)
```

```python
import functools
import math

import jax
import jax.numpy as jnp
from jax import lax
from jax.experimental import pallas as pl
from jax.experimental.pallas import tpu as pltpu
from jax.sharding import PartitionSpec as P

norm_eps = 1e-05
MESH = pl.DeviceIdType.MESH
f32, bf16, i32 = jnp.float32, jnp.bfloat16, jnp.int32
NT = (((1,), (1,)), ((), ()))
TN = (((0,), (0,)), ((), ()))
CHAIN_PAD = 8


def layer_norm(x, gain, shift):
    center = jnp.mean(x, axis=-1, keepdims=True)
    moved = x - center
    spread = jnp.mean(jnp.square(moved), axis=-1, keepdims=True)
    return moved * lax.rsqrt(spread + norm_eps) * gain + shift


def body(
    R, J, n, cols, heads, chains,
    first_ref, pairs_ref, vec_ref, src_hbm, w_hbm, bias_hbm, ow_hbm,
    out_hbm,
    src_v, norm_v, w_v, w_wide, wqvg_t, wk_t, ow_v,
    table_v, wanted_v, wanted_s, pos_v, pos_s,
    bias_all, bias_t,
    send_a0, send_a1, recv_a0, recv_a1,
    send_b0, send_b1, recv_b0, recv_b1,
    q_diag, att_v, send_c, gate_col,
    local_sem, idx_send, idx_recv, bias_send, bias_recv,
    a_send, a_recv, b_send, b0_recv, b1_recv, c_send, c_recv,
):
    L = n * J
    width = 256
    half = width // 2
    N = J * cols
    hd = width // heads
    Y = J // 2
    log2e = math.log2(math.e)
    me_r = lax.axis_index("rows")
    me_j = lax.axis_index("res")
    core = lax.rem(me_j, 2)

    def row_peer(t):
        return lax.rem(me_r + t, R)

    def res_peer(t):
        return lax.rem(me_j + t, J)

    load_src = pltpu.make_async_copy(src_hbm, src_v, local_sem.at[0])
    load_w = pltpu.make_async_copy(w_hbm, w_v, local_sem.at[1])
    load_bias = pltpu.make_async_copy(
        bias_hbm, bias_all.at[me_j // 2, core], local_sem.at[2]
    )
    load_ow = pltpu.make_async_copy(ow_hbm, ow_v, local_sem.at[3])
    load_src.start()
    load_bias.start()
    load_w.start()
    load_ow.start()

    barrier = pltpu.get_barrier_semaphore()

    @pl.loop(1, R)
    def _(t):
        pl.semaphore_signal(
            barrier, inc=1, device_id={"rows": row_peer(t)}, device_id_type=MESH
        )

    @pl.loop(1, J)
    def _(t):
        pl.semaphore_signal(
            barrier, inc=1, device_id={"res": res_peer(t)}, device_id_type=MESH
        )

    listed = pairs_ref[...]
    shift_bits = L.bit_length() - 1
    owner = lax.shift_right_arithmetic(listed, jnp.full_like(listed, shift_bits))
    within = jnp.bitwise_and(listed, L - 1)
    lane = lax.broadcasted_iota(i32, (R, 128), 1)
    row_id = lax.broadcasted_iota(i32, (R, L), 0)
    table = jnp.zeros((R, 128), i32)
    for c in range(chains):
        own_c = owner[c : c + 1, :]
        wit_c = within[c : c + 1, :]
        match = row_id == own_c
        low = jnp.min(jnp.where(match, wit_c, L), axis=1, keepdims=True)
        high = jnp.max(jnp.where(match, wit_c, -1), axis=1, keepdims=True)
        table = jnp.where(lane == c, jnp.minimum(low, L - 1), table)
        table = jnp.where(lane == CHAIN_PAD + c, jnp.maximum(high, 0), table)
        rank = jnp.max(
            jnp.where(match, jnp.where(wit_c > low, 1, 0), 0), axis=0, keepdims=True
        )
        pos_v[c : c + 1, 0:L] = jnp.where(own_c < 0, 2 * R, 2 * own_c + rank)
    table_v[...] = table.reshape(R, 1, 128)
    load_pos = pltpu.make_async_copy(pos_v, pos_s, local_sem.at[4])
    load_pos.start()

    col0 = me_j * cols
    chain_a = jnp.int32(0)
    chain_b = jnp.int32(0)
    for k in range(1, chains):
        chain_a += (first_ref[k] <= col0).astype(i32)
        chain_b += (first_ref[k] <= col0 + cols - 1).astype(i32)
    start_b = first_ref[chain_b] - col0
    in_b = lax.broadcasted_iota(i32, (cols, width), 0) >= start_b
    in_b_half = lax.broadcasted_iota(i32, (cols, half), 0) >= start_b

    pl.semaphore_wait(barrier, R - 1 + J - 1)

    wanted_v[me_r] = table_v[me_r]

    @pl.loop(1, R)
    def _(t):
        b = row_peer(t)
        pltpu.make_async_remote_copy(
            table_v.at[b], wanted_v.at[me_r], idx_send, idx_recv,
            device_id={"rows": b}, device_id_type=MESH,
        ).start()

    load_bias.wait()
    my_bias = bias_all.at[me_j // 2, core]

    @pl.loop(1, Y)
    def _(t):
        pltpu.make_async_remote_copy(
            my_bias, my_bias, bias_send.at[0], bias_recv.at[0],
            device_id={"res": res_peer(2 * t)}, device_id_type=MESH,
        ).start()

    gap = vec_ref[0:1, :]
    gain = vec_ref[1:2, :]
    shift = vec_ref[2:3, :]
    out_shift = vec_ref[3:4, :]
    load_src.wait()
    step = 4

    @pl.loop(0, L // step)
    def _(i):
        x = src_v[pl.ds(i * step, step)].astype(f32).reshape(step * cols, width)
        y = layer_norm(x, gain, shift).astype(bf16)
        norm_v[pl.ds(i * step, step)] = y.reshape(step, cols, width)

    gap_row = jnp.broadcast_to(layer_norm(gap, gain, shift), (cols, width)).astype(bf16)
    recv_a0[2 * R] = gap_row[:, :half]
    recv_a1[2 * R] = gap_row[:, half:]

    def wait_recv(ref, sem):
        pltpu.make_async_remote_copy(
            ref, ref, idx_send, sem, device_id={"rows": me_r}, device_id_type=MESH
        ).wait_recv()

    def wait_send(ref, sem):
        pltpu.make_async_remote_copy(
            ref, ref, sem, idx_recv, device_id={"rows": me_r}, device_id_type=MESH
        ).wait_send()

    wait_recv(wanted_v.at[pl.ds(0, R - 1)], idx_recv)
    load_wanted = pltpu.make_async_copy(wanted_v, wanted_s, local_sem.at[5])
    load_wanted.start()
    load_wanted.wait()
    load_pos.wait()

    def pick(b, k):
        at_a = jnp.clip(wanted_s[b, 0, k * CHAIN_PAD + chain_a], 0, L - 1)
        at_b = jnp.clip(wanted_s[b, 0, k * CHAIN_PAD + chain_b], 0, L - 1)
        return jnp.where(in_b, norm_v[at_b], norm_v[at_a])

    @pl.loop(1, R)
    def _(t):
        b = row_peer(t)
        for k in range(2):
            cells = pick(b, k)
            send_a0[b, k] = cells[:, :half]
            send_a1[b, k] = cells[:, half:]
        pltpu.make_async_remote_copy(
            send_a0.at[b], recv_a0.at[pl.ds(2 * me_r, 2)], a_send.at[0], a_recv.at[0],
            device_id={"rows": b}, device_id_type=MESH,
        ).start()

    @pl.loop(1, R)
    def _(t):
        b = row_peer(t)
        pltpu.make_async_remote_copy(
            send_a1.at[b], recv_a1.at[pl.ds(2 * me_r, 2)], a_send.at[1], a_recv.at[1],
            device_id={"rows": b}, device_id_type=MESH,
        ).start()

    for k in range(2):
        cells = pick(me_r, k)
        recv_a0[2 * me_r + k] = cells[:, :half]
        recv_a1[2 * me_r + k] = cells[:, half:]

    load_w.wait()
    load_ow.wait()
    w_wide[...] = w_v[...].astype(f32).reshape(width * heads, 128)
    q_diag[...] = jnp.zeros_like(q_diag)
    for h in range(heads):
        w_h = w_wide[pl.ds(h, width, stride=heads), :].T.astype(bf16)
        own = slice(h * hd, (h + 1) * hd)
        wqvg_t[0 * width + h * hd : 0 * width + (h + 1) * hd, :] = w_h[0:hd]
        wk_t[own, :] = w_h[hd : 2 * hd]
        wqvg_t[1 * width + h * hd : 1 * width + (h + 1) * hd, :] = w_h[2 * hd : 3 * hd]
        wqvg_t[2 * width + h * hd : 2 * width + (h + 1) * hd, :] = w_h[3 * hd :]
    gate_col[...] = jnp.broadcast_to(vec_ref[4:5, :], (128, width)).T

    wait_recv(recv_a0.at[pl.ds(0, 2 * (R - 1))], a_recv.at[0])

    def regather(recv, s):
        at_a = jnp.clip(pos_s[chain_a, s], 0, 2 * R)
        at_b = jnp.clip(pos_s[chain_b, s], 0, 2 * R)
        return jnp.where(in_b_half, recv[at_b], recv[at_a])

    @pl.loop(1, J)
    def _(t):
        j = res_peer(t)
        for r in range(n):
            send_b0[j, r] = regather(recv_a0, j * n + r)
        pltpu.make_async_remote_copy(
            send_b0.at[j], recv_b0.at[:, me_j], b_send.at[0], b0_recv,
            device_id={"res": j}, device_id_type=MESH,
        ).start()

    for r in range(n):
        recv_b0[r, me_j] = regather(recv_a0, me_j * n + r)

    wait_recv(bias_all.at[pl.ds(0, Y - 1), 0], bias_recv.at[0])
    share = bias_all.at[:, core]
    pltpu.make_async_remote_copy(
        share, share, bias_send.at[1], bias_recv.at[1],
        device_id={"res": me_j + 1 - 2 * core}, device_id_type=MESH,
    ).start()

    wait_recv(recv_a1.at[pl.ds(0, 2 * (R - 1))], a_recv.at[1])

    @pl.loop(0, n)
    def _(r):
        @pl.loop(1, J)
        def _(t):
            j = res_peer(t)
            send_b1[r, j] = regather(recv_a1, j * n + r)
            pltpu.make_async_remote_copy(
                send_b1.at[r, j], recv_b1.at[r, me_j], b_send.at[1], b1_recv.at[r],
                device_id={"res": j}, device_id_type=MESH,
            ).start()

        recv_b1[r, me_j] = regather(recv_a1, me_j * n + r)

    wait_recv(bias_all.at[:, 0], bias_recv.at[1])
    for h in range(heads):
        block = bias_all[:, :, h].reshape(N, N).astype(f32)
        bias_t[h] = block.T * log2e

    wait_recv(recv_b0.at[:, pl.ds(0, J - 1)], b0_recv)
    scale = hd ** (-0.5) * log2e

    @pl.loop(0, n)
    def _(r):
        wait_recv(recv_b1.at[r, pl.ds(0, J - 1)], b1_recv.at[r])
        x = jnp.concatenate(
            [recv_b0[r].reshape(N, half), recv_b1[r].reshape(N, half)], axis=1
        )
        qvg = lax.dot_general(wqvg_t[...], x, NT, preferred_element_type=f32)
        keys = lax.dot_general(x, wk_t[...], NT, preferred_element_type=f32).astype(bf16)
        q = (qvg[:width] * scale).astype(bf16)
        v = qvg[width : 2 * width].astype(bf16)
        gate = jax.nn.sigmoid(qvg[2 * width :] + gate_col[:, 0:1])
        ones = jnp.ones((16, N), bf16)
        for h in range(heads):
            own = slice(h * hd, (h + 1) * hd)
            q_diag[h, own, :] = q[own]
            s = jnp.dot(keys, q_diag[h], preferred_element_type=f32) + bias_t[h]
            top = jnp.max(s, axis=0, keepdims=True)
            e = jnp.exp2(s - top).astype(bf16)
            o = jnp.dot(
                jnp.concatenate([v[own], ones], axis=0), e, preferred_element_type=f32
            )
            att_v[own, :] = (o[:hd] * (1.0 / o[hd : hd + 1]) * gate[own]).astype(bf16)
        update = lax.dot_general(att_v[...], ow_v[...], TN, preferred_element_type=f32)
        update = (update + out_shift).astype(bf16)
        send_c[pl.ds(r * J, J)] = update.reshape(J, cols, width)

        @pl.loop(1, J)
        def _(t):
            j = res_peer(t)
            pltpu.make_async_remote_copy(
                send_c.at[r * J + j], out_hbm.at[me_j * n + r], c_send, c_recv,
                device_id={"res": j}, device_id_type=MESH,
            ).start()

        pltpu.make_async_copy(
            send_c.at[r * J + me_j], out_hbm.at[me_j * n + r], local_sem.at[6 + r]
        ).start()

    for r in range(n):
        pltpu.make_async_copy(
            send_c.at[r * J + me_j], out_hbm.at[me_j * n + r], local_sem.at[6 + r]
        ).wait()
    wait_send(table_v.at[pl.ds(0, R - 1)], idx_send)
    wait_send(bias_all.at[pl.ds(0, Y - 1), 0], bias_send.at[0])
    wait_send(bias_all.at[:, 0], bias_send.at[1])
    wait_send(send_a0.at[pl.ds(0, R - 1)], a_send.at[0])
    wait_send(send_a1.at[pl.ds(0, R - 1)], a_send.at[1])
    wait_send(send_b0.at[pl.ds(0, J - 1)], b_send.at[0])
    wait_send(send_b1.at[:, pl.ds(0, J - 1)], b_send.at[1])
    wait_send(send_c.at[pl.ds(0, n * (J - 1))], c_send)
    wait_recv(out_hbm.at[pl.ds(0, n * (J - 1))], c_recv)


def local(
    source_alignment_rows,
    pairs,
    chain_first_residue,
    gap_embedding,
    layer_norm_gain,
    layer_norm_bias,
    projection_weight,
    gate_bias_heads,
    pair_bias_logits,
    output_weight,
    output_bias,
):
    R, J = lax.axis_size("rows"), lax.axis_size("res")
    L, cols, width = source_alignment_rows.shape
    heads = projection_weight.shape[1]
    chains = pairs.shape[0]
    n = L // J
    N = J * cols
    half = width // 2
    vectors = jnp.stack(
        [gap_embedding, layer_norm_gain, layer_norm_bias, output_bias, gate_bias_heads]
    ).astype(f32)
    DMA = pltpu.SemaphoreType.DMA
    vmem, anywhere = pl.BlockSpec(memory_space=pltpu.VMEM), pl.BlockSpec(memory_space=pl.ANY)
    return pl.pallas_call(
        functools.partial(body, R, J, n, cols, heads, chains),
        out_shape=jax.ShapeDtypeStruct((L, cols, width), bf16),
        in_specs=[
            pl.BlockSpec(memory_space=pltpu.SMEM), vmem, vmem,
            anywhere, anywhere, anywhere, anywhere,
        ],
        out_specs=anywhere,
        scratch_shapes=[
            pltpu.VMEM((L, cols, width), bf16),
            pltpu.VMEM((L, cols, width), bf16),
            pltpu.VMEM((width, heads, 128), bf16),
            pltpu.VMEM((width * heads, 128), f32),
            pltpu.VMEM((3 * width, width), bf16),
            pltpu.VMEM((width, width), bf16),
            pltpu.VMEM((width, width), bf16),
            pltpu.VMEM((R, 1, 128), i32),
            pltpu.VMEM((R, 1, 128), i32),
            pltpu.SMEM((R, 1, 128), i32),
            pltpu.VMEM((8, 128), i32),
            pltpu.SMEM((8, 128), i32),
            pltpu.VMEM((J // 2, 2, heads, cols, N), bf16),
            pltpu.VMEM((heads, N, N), f32),
            pltpu.VMEM((R, 2, cols, half), bf16),
            pltpu.VMEM((R, 2, cols, half), bf16),
            pltpu.VMEM((2 * R + 1, cols, half), bf16),
            pltpu.VMEM((2 * R + 1, cols, half), bf16),
            pltpu.VMEM((J, n, cols, half), bf16),
            pltpu.VMEM((n, J, cols, half), bf16),
            pltpu.VMEM((n, J, cols, half), bf16),
            pltpu.VMEM((n, J, cols, half), bf16),
            pltpu.VMEM((heads, width, N), bf16),
            pltpu.VMEM((width, N), bf16),
            pltpu.VMEM((n * J, cols, width), bf16),
            pltpu.VMEM((width, 128), f32),
            DMA((6 + n,)), DMA, DMA, DMA((2,)), DMA((2,)),
            DMA((2,)), DMA((2,)), DMA((2,)), DMA, DMA((n,)), DMA, DMA,
        ],
        compiler_params=pltpu.CompilerParams(
            collective_id=0, has_side_effects=True, vmem_limit_bytes=40 * 1024 * 1024
        ),
    )(
        chain_first_residue, pairs, vectors, source_alignment_rows, projection_weight,
        pair_bias_logits, output_weight,
    )


def solution(mesh):
    return jax.shard_map(
        local,
        mesh=mesh,
        in_specs=(
            P("rows", "res", None),
            P(None, "rows"),
            P(),
            P(),
            P(),
            P(),
            P(),
            P(),
            P(None, "res", None),
            P(),
            P(),
        ),
        out_specs=P("rows", "res", None),
        check_vma=False,
    )
```

```python
import functools
import math

import jax
import jax.numpy as jnp
from jax import lax
from jax.experimental import pallas as pl
from jax.experimental.pallas import tpu as pltpu
from jax.sharding import PartitionSpec as P

norm_eps = 1e-05
MESH = pl.DeviceIdType.MESH
f32, bf16, i32 = jnp.float32, jnp.bfloat16, jnp.int32
NT = (((1,), (1,)), ((), ()))
TN = (((0,), (0,)), ((), ()))
CHAIN_PAD = 8


def layer_norm(x, gain, shift):
    center = jnp.mean(x, axis=-1, keepdims=True)
    moved = x - center
    spread = jnp.mean(jnp.square(moved), axis=-1, keepdims=True)
    return moved * lax.rsqrt(spread + norm_eps) * gain + shift


def body(
    R, J, n, cols, heads, chains,
    first_hbm, pairs_hbm, gap_hbm, gain_hbm, shift_hbm, out_shift_hbm, gate_hbm,
    src_hbm, w_hbm, bias_hbm, ow_hbm,
    out_hbm,
    first_ref, pairs_ref, vec_refs,
    src_v, norm_v, w_v, w_wide, wqvg_t, wk_t, ow_v,
    table_v, wanted_v, wanted_s, pos_v, pos_s,
    bias_all, bias_t,
    send_a0, send_a1, recv_a0, recv_a1,
    send_b0, send_b1, recv_b0, recv_b1,
    q_diag, att_v, send_c, gate_col,
    local_sem, idx_send, idx_recv, bias_send, bias_recv,
    a_send, a_recv, b_send, b0_recv, b1_recv, c_send, c_recv,
):
    L = n * J
    width = 256
    half = width // 2
    N = J * cols
    hd = width // heads
    Y = J // 2
    log2e = math.log2(math.e)
    me_r = lax.axis_index("rows")
    me_j = lax.axis_index("res")
    core = lax.rem(me_j, 2)

    def row_peer(t):
        return lax.rem(me_r + t, R)

    def res_peer(t):
        return lax.rem(me_j + t, J)

    load_src = pltpu.make_async_copy(src_hbm, src_v, local_sem.at[0])
    load_w = pltpu.make_async_copy(w_hbm, w_v, local_sem.at[1])
    load_bias = pltpu.make_async_copy(
        bias_hbm, bias_all.at[me_j // 2, core], local_sem.at[2]
    )
    load_ow = pltpu.make_async_copy(ow_hbm, ow_v, local_sem.at[3])
    load_first = pltpu.make_async_copy(first_hbm, first_ref, local_sem.at[6])
    load_pairs = pltpu.make_async_copy(pairs_hbm, pairs_ref, local_sem.at[7])
    load_vecs = [
        pltpu.make_async_copy(v, vec_refs[i], local_sem.at[8 + i])
        for i, v in enumerate([gap_hbm, gain_hbm, shift_hbm, out_shift_hbm, gate_hbm])
    ]
    load_pairs.start()
    load_first.start()
    load_src.start()
    for load in load_vecs:
        load.start()
    load_bias.start()
    load_w.start()
    load_ow.start()

    barrier = pltpu.get_barrier_semaphore()

    @pl.loop(1, R)
    def _(t):
        pl.semaphore_signal(
            barrier, inc=1, device_id={"rows": row_peer(t)}, device_id_type=MESH
        )

    @pl.loop(1, J)
    def _(t):
        pl.semaphore_signal(
            barrier, inc=1, device_id={"res": res_peer(t)}, device_id_type=MESH
        )

    load_pairs.wait()
    listed = pairs_ref[...]
    shift_bits = L.bit_length() - 1
    owner = lax.shift_right_arithmetic(listed, jnp.full_like(listed, shift_bits))
    within = jnp.bitwise_and(listed, L - 1)
    lane = lax.broadcasted_iota(i32, (R, 128), 1)
    row_id = lax.broadcasted_iota(i32, (R, L), 0)
    table = jnp.zeros((R, 128), i32)
    for c in range(chains):
        own_c = owner[c : c + 1, :]
        wit_c = within[c : c + 1, :]
        match = row_id == own_c
        low = jnp.min(jnp.where(match, wit_c, L), axis=1, keepdims=True)
        high = jnp.max(jnp.where(match, wit_c, -1), axis=1, keepdims=True)
        table = jnp.where(lane == c, jnp.minimum(low, L - 1), table)
        table = jnp.where(lane == CHAIN_PAD + c, jnp.maximum(high, 0), table)
        rank = jnp.max(
            jnp.where(match, jnp.where(wit_c > low, 1, 0), 0), axis=0, keepdims=True
        )
        pos_v[c : c + 1, 0:L] = jnp.where(own_c < 0, 2 * R, 2 * own_c + rank)
    table_v[...] = table.reshape(R, 1, 128)
    load_pos = pltpu.make_async_copy(pos_v, pos_s, local_sem.at[4])
    load_pos.start()

    load_first.wait()
    col0 = me_j * cols
    chain_a = jnp.int32(0)
    chain_b = jnp.int32(0)
    for k in range(1, chains):
        chain_a += (first_ref[k] <= col0).astype(i32)
        chain_b += (first_ref[k] <= col0 + cols - 1).astype(i32)
    start_b = first_ref[chain_b] - col0
    in_b = lax.broadcasted_iota(i32, (cols, width), 0) >= start_b
    in_b_half = lax.broadcasted_iota(i32, (cols, half), 0) >= start_b

    pl.semaphore_wait(barrier, R - 1 + J - 1)

    wanted_v[me_r] = table_v[me_r]

    @pl.loop(1, R)
    def _(t):
        b = row_peer(t)
        pltpu.make_async_remote_copy(
            table_v.at[b], wanted_v.at[me_r], idx_send, idx_recv,
            device_id={"rows": b}, device_id_type=MESH,
        ).start()

    load_bias.wait()
    my_bias = bias_all.at[me_j // 2, core]

    @pl.loop(1, Y)
    def _(t):
        pltpu.make_async_remote_copy(
            my_bias, my_bias, bias_send.at[0], bias_recv.at[0],
            device_id={"res": res_peer(2 * t)}, device_id_type=MESH,
        ).start()

    for load in load_vecs:
        load.wait()
    gap, gain, shift, out_shift, gate_shift = [
        v[...].astype(f32).reshape(1, width) for v in vec_refs
    ]
    load_src.wait()
    step = 4

    @pl.loop(0, L // step)
    def _(i):
        x = src_v[pl.ds(i * step, step)].astype(f32).reshape(step * cols, width)
        y = layer_norm(x, gain, shift).astype(bf16)
        norm_v[pl.ds(i * step, step)] = y.reshape(step, cols, width)

    gap_row = jnp.broadcast_to(layer_norm(gap, gain, shift), (cols, width)).astype(bf16)
    recv_a0[2 * R] = gap_row[:, :half]
    recv_a1[2 * R] = gap_row[:, half:]

    def wait_recv(ref, sem):
        pltpu.make_async_remote_copy(
            ref, ref, idx_send, sem, device_id={"rows": me_r}, device_id_type=MESH
        ).wait_recv()

    def wait_send(ref, sem):
        pltpu.make_async_remote_copy(
            ref, ref, sem, idx_recv, device_id={"rows": me_r}, device_id_type=MESH
        ).wait_send()

    wait_recv(wanted_v.at[pl.ds(0, R - 1)], idx_recv)
    load_wanted = pltpu.make_async_copy(wanted_v, wanted_s, local_sem.at[5])
    load_wanted.start()
    load_wanted.wait()
    load_pos.wait()

    def pick(b, k):
        at_a = jnp.clip(wanted_s[b, 0, k * CHAIN_PAD + chain_a], 0, L - 1)
        at_b = jnp.clip(wanted_s[b, 0, k * CHAIN_PAD + chain_b], 0, L - 1)
        return jnp.where(in_b, norm_v[at_b], norm_v[at_a])

    @pl.loop(1, R)
    def _(t):
        b = row_peer(t)
        for k in range(2):
            cells = pick(b, k)
            send_a0[b, k] = cells[:, :half]
            send_a1[b, k] = cells[:, half:]
        pltpu.make_async_remote_copy(
            send_a0.at[b], recv_a0.at[pl.ds(2 * me_r, 2)], a_send.at[0], a_recv.at[0],
            device_id={"rows": b}, device_id_type=MESH,
        ).start()

    @pl.loop(1, R)
    def _(t):
        b = row_peer(t)
        pltpu.make_async_remote_copy(
            send_a1.at[b], recv_a1.at[pl.ds(2 * me_r, 2)], a_send.at[1], a_recv.at[1],
            device_id={"rows": b}, device_id_type=MESH,
        ).start()

    for k in range(2):
        cells = pick(me_r, k)
        recv_a0[2 * me_r + k] = cells[:, :half]
        recv_a1[2 * me_r + k] = cells[:, half:]

    load_w.wait()
    load_ow.wait()
    w_wide[...] = w_v[...].astype(f32).reshape(width * heads, 128)
    q_diag[...] = jnp.zeros_like(q_diag)
    for h in range(heads):
        w_h = w_wide[pl.ds(h, width, stride=heads), :].T.astype(bf16)
        own = slice(h * hd, (h + 1) * hd)
        wqvg_t[0 * width + h * hd : 0 * width + (h + 1) * hd, :] = w_h[0:hd]
        wk_t[own, :] = w_h[hd : 2 * hd]
        wqvg_t[1 * width + h * hd : 1 * width + (h + 1) * hd, :] = w_h[2 * hd : 3 * hd]
        wqvg_t[2 * width + h * hd : 2 * width + (h + 1) * hd, :] = w_h[3 * hd :]
    gate_col[...] = jnp.broadcast_to(gate_shift, (128, width)).T

    wait_recv(recv_a0.at[pl.ds(0, 2 * (R - 1))], a_recv.at[0])

    def regather(recv, s):
        at_a = jnp.clip(pos_s[chain_a, s], 0, 2 * R)
        at_b = jnp.clip(pos_s[chain_b, s], 0, 2 * R)
        return jnp.where(in_b_half, recv[at_b], recv[at_a])

    @pl.loop(1, J)
    def _(t):
        j = res_peer(t)
        for r in range(n):
            send_b0[j, r] = regather(recv_a0, j * n + r)
        pltpu.make_async_remote_copy(
            send_b0.at[j], recv_b0.at[:, me_j], b_send.at[0], b0_recv,
            device_id={"res": j}, device_id_type=MESH,
        ).start()

    for r in range(n):
        recv_b0[r, me_j] = regather(recv_a0, me_j * n + r)

    wait_recv(bias_all.at[pl.ds(0, Y - 1), 0], bias_recv.at[0])
    share = bias_all.at[:, core]
    pltpu.make_async_remote_copy(
        share, share, bias_send.at[1], bias_recv.at[1],
        device_id={"res": me_j + 1 - 2 * core}, device_id_type=MESH,
    ).start()

    wait_recv(recv_a1.at[pl.ds(0, 2 * (R - 1))], a_recv.at[1])

    @pl.loop(0, n)
    def _(r):
        @pl.loop(1, J)
        def _(t):
            j = res_peer(t)
            send_b1[r, j] = regather(recv_a1, j * n + r)
            pltpu.make_async_remote_copy(
                send_b1.at[r, j], recv_b1.at[r, me_j], b_send.at[1], b1_recv.at[r],
                device_id={"res": j}, device_id_type=MESH,
            ).start()

        recv_b1[r, me_j] = regather(recv_a1, me_j * n + r)

    wait_recv(bias_all.at[:, 0], bias_recv.at[1])
    for h in range(heads):
        block = bias_all[:, :, h].reshape(N, N).astype(f32)
        bias_t[h] = block.T * log2e

    wait_recv(recv_b0.at[:, pl.ds(0, J - 1)], b0_recv)
    scale = hd ** (-0.5) * log2e

    @pl.loop(0, n)
    def _(r):
        wait_recv(recv_b1.at[r, pl.ds(0, J - 1)], b1_recv.at[r])
        x = jnp.concatenate(
            [recv_b0[r].reshape(N, half), recv_b1[r].reshape(N, half)], axis=1
        )
        qvg = lax.dot_general(wqvg_t[...], x, NT, preferred_element_type=f32)
        keys = lax.dot_general(x, wk_t[...], NT, preferred_element_type=f32).astype(bf16)
        q = (qvg[:width] * scale).astype(bf16)
        v = qvg[width : 2 * width].astype(bf16)
        gate = jax.nn.sigmoid(qvg[2 * width :] + gate_col[:, 0:1])
        ones = jnp.ones((16, N), bf16)
        for h in range(heads):
            own = slice(h * hd, (h + 1) * hd)
            q_diag[h, own, :] = q[own]
            s = jnp.dot(keys, q_diag[h], preferred_element_type=f32) + bias_t[h]
            top = jnp.max(s, axis=0, keepdims=True)
            e = jnp.exp2(s - top).astype(bf16)
            o = jnp.dot(
                jnp.concatenate([v[own], ones], axis=0), e, preferred_element_type=f32
            )
            att_v[own, :] = (o[:hd] * (1.0 / o[hd : hd + 1]) * gate[own]).astype(bf16)
        update = lax.dot_general(att_v[...], ow_v[...], TN, preferred_element_type=f32)
        update = (update + out_shift).astype(bf16)
        send_c[pl.ds(r * J, J)] = update.reshape(J, cols, width)

        @pl.loop(1, J)
        def _(t):
            j = res_peer(t)
            pltpu.make_async_remote_copy(
                send_c.at[r * J + j], out_hbm.at[me_j * n + r], c_send, c_recv,
                device_id={"res": j}, device_id_type=MESH,
            ).start()

        pltpu.make_async_copy(
            send_c.at[r * J + me_j], out_hbm.at[me_j * n + r], local_sem.at[13 + r]
        ).start()

    for r in range(n):
        pltpu.make_async_copy(
            send_c.at[r * J + me_j], out_hbm.at[me_j * n + r], local_sem.at[13 + r]
        ).wait()
    wait_send(table_v.at[pl.ds(0, R - 1)], idx_send)
    wait_send(bias_all.at[pl.ds(0, Y - 1), 0], bias_send.at[0])
    wait_send(bias_all.at[:, 0], bias_send.at[1])
    wait_send(send_a0.at[pl.ds(0, R - 1)], a_send.at[0])
    wait_send(send_a1.at[pl.ds(0, R - 1)], a_send.at[1])
    wait_send(send_b0.at[pl.ds(0, J - 1)], b_send.at[0])
    wait_send(send_b1.at[:, pl.ds(0, J - 1)], b_send.at[1])
    wait_send(send_c.at[pl.ds(0, n * (J - 1))], c_send)
    wait_recv(out_hbm.at[pl.ds(0, n * (J - 1))], c_recv)


def local(
    source_alignment_rows,
    pairs,
    chain_first_residue,
    gap_embedding,
    layer_norm_gain,
    layer_norm_bias,
    projection_weight,
    gate_bias_heads,
    pair_bias_logits,
    output_weight,
    output_bias,
):
    R, J = lax.axis_size("rows"), lax.axis_size("res")
    L, cols, width = source_alignment_rows.shape
    heads = projection_weight.shape[1]
    chains = pairs.shape[0]
    n = L // J
    N = J * cols
    half = width // 2
    DMA = pltpu.SemaphoreType.DMA
    hbm = pl.BlockSpec(memory_space=pltpu.HBM)
    return pl.pallas_call(
        functools.partial(body, R, J, n, cols, heads, chains),
        out_shape=jax.ShapeDtypeStruct((L, cols, width), bf16),
        in_specs=[hbm] * 11,
        out_specs=hbm,
        scratch_shapes=[
            pltpu.SMEM((chains,), i32),
            pltpu.VMEM((chains, L), i32),
            [pltpu.VMEM((width,), bf16)] * 5,
            pltpu.VMEM((L, cols, width), bf16),
            pltpu.VMEM((L, cols, width), bf16),
            pltpu.VMEM((width, heads, 128), bf16),
            pltpu.VMEM((width * heads, 128), f32),
            pltpu.VMEM((3 * width, width), bf16),
            pltpu.VMEM((width, width), bf16),
            pltpu.VMEM((width, width), bf16),
            pltpu.VMEM((R, 1, 128), i32),
            pltpu.VMEM((R, 1, 128), i32),
            pltpu.SMEM((R, 1, 128), i32),
            pltpu.VMEM((8, 128), i32),
            pltpu.SMEM((8, 128), i32),
            pltpu.VMEM((J // 2, 2, heads, cols, N), bf16),
            pltpu.VMEM((heads, N, N), f32),
            pltpu.VMEM((R, 2, cols, half), bf16),
            pltpu.VMEM((R, 2, cols, half), bf16),
            pltpu.VMEM((2 * R + 1, cols, half), bf16),
            pltpu.VMEM((2 * R + 1, cols, half), bf16),
            pltpu.VMEM((J, n, cols, half), bf16),
            pltpu.VMEM((n, J, cols, half), bf16),
            pltpu.VMEM((n, J, cols, half), bf16),
            pltpu.VMEM((n, J, cols, half), bf16),
            pltpu.VMEM((heads, width, N), bf16),
            pltpu.VMEM((width, N), bf16),
            pltpu.VMEM((n * J, cols, width), bf16),
            pltpu.VMEM((width, 128), f32),
            DMA((13 + n,)), DMA, DMA, DMA((2,)), DMA((2,)),
            DMA((2,)), DMA((2,)), DMA((2,)), DMA, DMA((n,)), DMA, DMA,
        ],
        compiler_params=pltpu.CompilerParams(
            collective_id=0, has_side_effects=True, vmem_limit_bytes=63 * 1024 * 1024
        ),
    )(
        chain_first_residue, pairs, gap_embedding, layer_norm_gain,
        layer_norm_bias, output_bias, gate_bias_heads,
        source_alignment_rows, projection_weight, pair_bias_logits, output_weight,
    )


def solution(mesh):
    return jax.shard_map(
        local,
        mesh=mesh,
        in_specs=(
            P("rows", "res", None),
            P(None, "rows"),
            P(),
            P(),
            P(),
            P(),
            P(),
            P(),
            P(None, "res", None),
            P(),
            P(),
        ),
        out_specs=P("rows", "res", None),
        check_vma=False,
    )
```

```python
import functools
import math

import jax
import jax.numpy as jnp
from jax import lax
from jax.experimental import pallas as pl
from jax.experimental.pallas import tpu as pltpu
from jax.sharding import PartitionSpec as P

norm_eps = 1e-05
MESH = pl.DeviceIdType.MESH
f32, bf16, i32 = jnp.float32, jnp.bfloat16, jnp.int32
NT = (((1,), (1,)), ((), ()))
TN = (((0,), (0,)), ((), ()))
CHAIN_PAD = 8


def layer_norm(x, gain, shift):
    center = jnp.mean(x, axis=-1, keepdims=True)
    moved = x - center
    spread = jnp.mean(jnp.square(moved), axis=-1, keepdims=True)
    return moved * lax.rsqrt(spread + norm_eps) * gain + shift


def body(
    R, J, n, cols, heads, chains,
    first_hbm, pairs_hbm, gap_hbm, gain_hbm, shift_hbm, out_shift_hbm, gate_hbm,
    src_hbm, w_hbm, bias_hbm, ow_hbm,
    out_hbm,
    first_ref, pairs_ref, vec_refs,
    src_v, norm_v, w_v, w_wide, wqvg_t, wk_t, ow_v,
    table_v, wanted_v, wanted_s, pos_v, pos_s,
    bias_all, bias_t,
    send_a0, send_a1, recv_a0, recv_a1,
    send_b0, send_b1, recv_b0, recv_b1,
    q_diag, att_v, send_c, gate_col, score_v, lifted_v, v_ext, gate_v,
    local_sem, idx_send, idx_recv, bias_send, bias_recv,
    a_send, a_recv, b_send, b0_recv, b1_recv, c_send, c_recv,
):
    L = n * J
    width = 256
    half = width // 2
    N = J * cols
    hd = width // heads
    Y = J // 2
    log2e = math.log2(math.e)
    me_r = lax.axis_index("rows")
    me_j = lax.axis_index("res")
    core = lax.rem(me_j, 2)

    X = 4
    Z = R // X
    me_z, me_x = me_r // X, lax.rem(me_r, X)

    def farthest_first(size, i):
        odd = lax.rem(i, 2)
        return size // 2 + (1 - 2 * odd) * ((i + odd) // 2)

    def row_peer(t):
        z = lax.rem(me_z + farthest_first(Z, t // X), Z)
        x = lax.rem(me_x + farthest_first(X, lax.rem(t, X)), X)
        return z * X + x

    def res_peer(t):
        y = lax.rem(me_j // 2 + farthest_first(Y, t // 2), Y)
        return 2 * y + lax.rem(core + 1 + lax.rem(t, 2), 2)

    load_src = pltpu.make_async_copy(src_hbm, src_v, local_sem.at[0])
    load_w = pltpu.make_async_copy(w_hbm, w_v, local_sem.at[1])
    load_bias = pltpu.make_async_copy(
        bias_hbm, bias_all.at[me_j // 2, core], local_sem.at[2]
    )
    load_ow = pltpu.make_async_copy(ow_hbm, ow_v, local_sem.at[3])
    load_first = pltpu.make_async_copy(first_hbm, first_ref, local_sem.at[6])
    load_pairs = pltpu.make_async_copy(pairs_hbm, pairs_ref, local_sem.at[7])
    load_vecs = [
        pltpu.make_async_copy(v, vec_refs[i], local_sem.at[8 + i])
        for i, v in enumerate([gap_hbm, gain_hbm, shift_hbm, out_shift_hbm, gate_hbm])
    ]
    load_pairs.start()
    load_first.start()
    load_src.start()
    for load in load_vecs:
        load.start()
    load_bias.start()
    load_w.start()
    load_ow.start()

    barrier = pltpu.get_barrier_semaphore()

    @pl.loop(0, R - 1)
    def _(t):
        pl.semaphore_signal(
            barrier, inc=1, device_id={"rows": row_peer(t)}, device_id_type=MESH
        )

    @pl.loop(0, J - 1)
    def _(t):
        pl.semaphore_signal(
            barrier, inc=1, device_id={"res": res_peer(t)}, device_id_type=MESH
        )

    load_pairs.wait()
    listed = pairs_ref[...]
    shift_bits = L.bit_length() - 1
    owner = lax.shift_right_arithmetic(listed, jnp.full_like(listed, shift_bits))
    within = jnp.bitwise_and(listed, L - 1)
    lane = lax.broadcasted_iota(i32, (R, 128), 1)
    row_id = lax.broadcasted_iota(i32, (R, L), 0)
    table = jnp.zeros((R, 128), i32)
    for c in range(chains):
        own_c = owner[c : c + 1, :]
        wit_c = within[c : c + 1, :]
        match = row_id == own_c
        low = jnp.min(jnp.where(match, wit_c, L), axis=1, keepdims=True)
        high = jnp.max(jnp.where(match, wit_c, -1), axis=1, keepdims=True)
        table = jnp.where(lane == c, jnp.minimum(low, L - 1), table)
        table = jnp.where(lane == CHAIN_PAD + c, jnp.maximum(high, 0), table)
        rank = jnp.max(
            jnp.where(match, jnp.where(wit_c > low, 1, 0), 0), axis=0, keepdims=True
        )
        pos_v[c : c + 1, 0:L] = jnp.where(own_c < 0, 2 * R, 2 * own_c + rank)
    table_v[...] = table.reshape(R, 1, 128)
    load_pos = pltpu.make_async_copy(pos_v, pos_s, local_sem.at[4])
    load_pos.start()

    load_first.wait()
    col0 = me_j * cols
    chain_a = jnp.int32(0)
    chain_b = jnp.int32(0)
    for k in range(1, chains):
        chain_a += (first_ref[k] <= col0).astype(i32)
        chain_b += (first_ref[k] <= col0 + cols - 1).astype(i32)
    start_b = first_ref[chain_b] - col0
    in_b = lax.broadcasted_iota(i32, (cols, width), 0) >= start_b
    in_b_half = lax.broadcasted_iota(i32, (cols, half), 0) >= start_b

    pl.semaphore_wait(barrier, R - 1 + J - 1)

    wanted_v[me_r] = table_v[me_r]

    @pl.loop(0, R - 1)
    def _(t):
        b = row_peer(t)
        pltpu.make_async_remote_copy(
            table_v.at[b], wanted_v.at[me_r], idx_send, idx_recv,
            device_id={"rows": b}, device_id_type=MESH,
        ).start()

    load_bias.wait()
    my_bias = bias_all.at[me_j // 2, core]

    @pl.loop(0, Y - 1)
    def _(t):
        pltpu.make_async_remote_copy(
            my_bias, my_bias, bias_send.at[0], bias_recv.at[0],
            device_id={"res": res_peer(2 * t + 1)}, device_id_type=MESH,
        ).start()

    for load in load_vecs:
        load.wait()
    gap, gain, shift, out_shift, gate_shift = [
        v[...].astype(f32).reshape(1, width) for v in vec_refs
    ]
    load_src.wait()
    step = 4

    @pl.loop(0, L // step)
    def _(i):
        x = src_v[pl.ds(i * step, step)].astype(f32).reshape(step * cols, width)
        y = layer_norm(x, gain, shift).astype(bf16)
        norm_v[pl.ds(i * step, step)] = y.reshape(step, cols, width)

    gap_row = jnp.broadcast_to(layer_norm(gap, gain, shift), (cols, width)).astype(bf16)
    recv_a0[2 * R] = gap_row[:, :half]
    recv_a1[2 * R] = gap_row[:, half:]

    def wait_recv(ref, sem):
        pltpu.make_async_remote_copy(
            ref, ref, idx_send, sem, device_id={"rows": me_r}, device_id_type=MESH
        ).wait_recv()

    def wait_send(ref, sem):
        pltpu.make_async_remote_copy(
            ref, ref, sem, idx_recv, device_id={"rows": me_r}, device_id_type=MESH
        ).wait_send()

    wait_recv(wanted_v.at[pl.ds(0, R - 1)], idx_recv)
    load_wanted = pltpu.make_async_copy(wanted_v, wanted_s, local_sem.at[5])
    load_wanted.start()
    load_wanted.wait()
    load_pos.wait()

    def pick(b, k):
        at_a = jnp.clip(wanted_s[b, 0, k * CHAIN_PAD + chain_a], 0, L - 1)
        at_b = jnp.clip(wanted_s[b, 0, k * CHAIN_PAD + chain_b], 0, L - 1)
        return jnp.where(in_b, norm_v[at_b], norm_v[at_a])

    @pl.loop(0, R - 1)
    def _(t):
        b = row_peer(t)
        for k in range(2):
            cells = pick(b, k)
            send_a0[b, k] = cells[:, :half]
            send_a1[b, k] = cells[:, half:]
        pltpu.make_async_remote_copy(
            send_a0.at[b], recv_a0.at[pl.ds(2 * me_r, 2)], a_send.at[0], a_recv.at[0],
            device_id={"rows": b}, device_id_type=MESH,
        ).start()

    @pl.loop(0, R - 1)
    def _(t):
        b = row_peer(t)
        pltpu.make_async_remote_copy(
            send_a1.at[b], recv_a1.at[pl.ds(2 * me_r, 2)], a_send.at[1], a_recv.at[1],
            device_id={"rows": b}, device_id_type=MESH,
        ).start()

    for k in range(2):
        cells = pick(me_r, k)
        recv_a0[2 * me_r + k] = cells[:, :half]
        recv_a1[2 * me_r + k] = cells[:, half:]

    load_w.wait()
    load_ow.wait()
    w_wide[...] = w_v[...].astype(f32).reshape(width * heads, 128)
    q_diag[...] = jnp.zeros_like(q_diag)
    v_ext[...] = jnp.ones_like(v_ext)

    @pl.loop(0, heads)
    def _(h):
        w_h = w_wide[pl.ds(h, width, stride=heads), :].T.astype(bf16)
        wqvg_t[0, h] = w_h[0:hd]
        wk_t[h] = w_h[hd : 2 * hd]
        wqvg_t[1, h] = w_h[2 * hd : 3 * hd]
        wqvg_t[2, h] = w_h[3 * hd :]

    gate_col[...] = jnp.broadcast_to(gate_shift, (128, width)).T

    wait_recv(recv_a0.at[pl.ds(0, 2 * (R - 1))], a_recv.at[0])

    def regather(recv, s):
        at_a = jnp.clip(pos_s[chain_a, s], 0, 2 * R)
        at_b = jnp.clip(pos_s[chain_b, s], 0, 2 * R)
        return jnp.where(in_b_half, recv[at_b], recv[at_a])

    @pl.loop(0, J - 1)
    def _(t):
        j = res_peer(t)
        for r in range(n):
            send_b0[j, r] = regather(recv_a0, j * n + r)
        pltpu.make_async_remote_copy(
            send_b0.at[j], recv_b0.at[:, me_j], b_send.at[0], b0_recv,
            device_id={"res": j}, device_id_type=MESH,
        ).start()

    for r in range(n):
        recv_b0[r, me_j] = regather(recv_a0, me_j * n + r)

    wait_recv(bias_all.at[pl.ds(0, Y - 1), 0], bias_recv.at[0])
    share = bias_all.at[:, core]
    pltpu.make_async_remote_copy(
        share, share, bias_send.at[1], bias_recv.at[1],
        device_id={"res": me_j + 1 - 2 * core}, device_id_type=MESH,
    ).start()

    wait_recv(recv_a1.at[pl.ds(0, 2 * (R - 1))], a_recv.at[1])

    @pl.loop(0, n)
    def _(r):
        @pl.loop(0, J - 1)
        def _(t):
            j = res_peer(t)
            send_b1[r, j] = regather(recv_a1, j * n + r)
            pltpu.make_async_remote_copy(
                send_b1.at[r, j], recv_b1.at[r, me_j], b_send.at[1], b1_recv.at[r],
                device_id={"res": j}, device_id_type=MESH,
            ).start()

        recv_b1[r, me_j] = regather(recv_a1, me_j * n + r)

    wait_recv(bias_all.at[:, 0], bias_recv.at[1])

    @pl.loop(0, heads)
    def _(h):
        block = bias_all[:, :, h].reshape(N, N).astype(f32)
        bias_t[h] = block.T * log2e

    wait_recv(recv_b0.at[:, pl.ds(0, J - 1)], b0_recv)
    scale = hd ** (-0.5) * log2e

    @pl.loop(0, n)
    def _(r):
        wait_recv(recv_b1.at[r, pl.ds(0, J - 1)], b1_recv.at[r])
        x = jnp.concatenate(
            [recv_b0[r].reshape(N, half), recv_b1[r].reshape(N, half)], axis=1
        )
        qvg = lax.dot_general(
            wqvg_t[...].reshape(3 * width, width), x, NT, preferred_element_type=f32
        )
        keys = lax.dot_general(
            x, wk_t[...].reshape(width, width), NT, preferred_element_type=f32
        ).astype(bf16)
        q = (qvg[:width] * scale).astype(bf16)
        v = qvg[width : 2 * width].astype(bf16)
        gate_v[...] = jax.nn.sigmoid(qvg[2 * width :] + gate_col[:, 0:1])
        for h in range(heads):
            own = slice(h * hd, (h + 1) * hd)
            q_diag[own, h * N : (h + 1) * N] = q[own]
            v_ext[h, :hd, :] = v[own]
        score_v[...] = jnp.dot(keys, q_diag[...], preferred_element_type=f32)
        part = min(N, 128)
        for t in range(heads * N // part):
            h, at = t * part // N, t * part % N
            s = score_v[:, t * part : (t + 1) * part] + bias_t[h, :, at : at + part]
            top = jnp.max(s, axis=0, keepdims=True)
            lifted_v[:, t * part : (t + 1) * part] = jnp.exp2(s - top).astype(bf16)
        for h in range(heads):
            own = slice(h * hd, (h + 1) * hd)
            o = jnp.dot(
                v_ext[h], lifted_v[:, h * N : (h + 1) * N], preferred_element_type=f32
            )
            att_v[own, :] = (o[:hd] * (1.0 / o[hd : hd + 1]) * gate_v[own]).astype(bf16)
        update = lax.dot_general(att_v[...], ow_v[...], TN, preferred_element_type=f32)
        update = (update + out_shift).astype(bf16)
        send_c[pl.ds(r * J, J)] = update.reshape(J, cols, width)

        @pl.loop(0, J - 1)
        def _(t):
            j = res_peer(t)
            pltpu.make_async_remote_copy(
                send_c.at[r * J + j], out_hbm.at[me_j * n + r], c_send, c_recv,
                device_id={"res": j}, device_id_type=MESH,
            ).start()

        pltpu.make_async_copy(
            send_c.at[r * J + me_j], out_hbm.at[me_j * n + r], local_sem.at[13 + r]
        ).start()

    for r in range(n):
        pltpu.make_async_copy(
            send_c.at[r * J + me_j], out_hbm.at[me_j * n + r], local_sem.at[13 + r]
        ).wait()
    wait_send(table_v.at[pl.ds(0, R - 1)], idx_send)
    wait_send(bias_all.at[pl.ds(0, Y - 1), 0], bias_send.at[0])
    wait_send(bias_all.at[:, 0], bias_send.at[1])
    wait_send(send_a0.at[pl.ds(0, R - 1)], a_send.at[0])
    wait_send(send_a1.at[pl.ds(0, R - 1)], a_send.at[1])
    wait_send(send_b0.at[pl.ds(0, J - 1)], b_send.at[0])
    wait_send(send_b1.at[:, pl.ds(0, J - 1)], b_send.at[1])
    wait_send(send_c.at[pl.ds(0, n * (J - 1))], c_send)
    wait_recv(out_hbm.at[pl.ds(0, n * (J - 1))], c_recv)


def local(
    source_alignment_rows,
    pairs,
    chain_first_residue,
    gap_embedding,
    layer_norm_gain,
    layer_norm_bias,
    projection_weight,
    gate_bias_heads,
    pair_bias_logits,
    output_weight,
    output_bias,
):
    R, J = lax.axis_size("rows"), lax.axis_size("res")
    L, cols, width = source_alignment_rows.shape
    heads = projection_weight.shape[1]
    chains = pairs.shape[0]
    n = L // J
    N = J * cols
    half = width // 2
    DMA = pltpu.SemaphoreType.DMA
    hbm = pl.BlockSpec(memory_space=pltpu.HBM)
    return pl.pallas_call(
        functools.partial(body, R, J, n, cols, heads, chains),
        out_shape=jax.ShapeDtypeStruct((L, cols, width), bf16),
        in_specs=[hbm] * 11,
        out_specs=hbm,
        scratch_shapes=[
            pltpu.SMEM((chains,), i32),
            pltpu.VMEM((chains, L), i32),
            [pltpu.VMEM((width,), bf16)] * 5,
            pltpu.VMEM((L, cols, width), bf16),
            pltpu.VMEM((L, cols, width), bf16),
            pltpu.VMEM((width, heads, 128), bf16),
            pltpu.VMEM((width * heads, 128), f32),
            pltpu.VMEM((3, heads, width // heads, width), bf16),
            pltpu.VMEM((heads, width // heads, width), bf16),
            pltpu.VMEM((width, width), bf16),
            pltpu.VMEM((R, 1, 128), i32),
            pltpu.VMEM((R, 1, 128), i32),
            pltpu.SMEM((R, 1, 128), i32),
            pltpu.VMEM((8, 128), i32),
            pltpu.SMEM((8, 128), i32),
            pltpu.VMEM((J // 2, 2, heads, cols, N), bf16),
            pltpu.VMEM((heads, N, N), f32),
            pltpu.VMEM((R, 2, cols, half), bf16),
            pltpu.VMEM((R, 2, cols, half), bf16),
            pltpu.VMEM((2 * R + 1, cols, half), bf16),
            pltpu.VMEM((2 * R + 1, cols, half), bf16),
            pltpu.VMEM((J, n, cols, half), bf16),
            pltpu.VMEM((n, J, cols, half), bf16),
            pltpu.VMEM((n, J, cols, half), bf16),
            pltpu.VMEM((n, J, cols, half), bf16),
            pltpu.VMEM((width, heads * N), bf16),
            pltpu.VMEM((width, N), bf16),
            pltpu.VMEM((n * J, cols, width), bf16),
            pltpu.VMEM((width, 128), f32),
            pltpu.VMEM((N, heads * N), f32),
            pltpu.VMEM((N, heads * N), bf16),
            pltpu.VMEM((heads, width // heads + 16, N), bf16),
            pltpu.VMEM((width, N), f32),
            DMA((13 + n,)), DMA, DMA, DMA((2,)), DMA((2,)),
            DMA((2,)), DMA((2,)), DMA((2,)), DMA, DMA((n,)), DMA, DMA,
        ],
        compiler_params=pltpu.CompilerParams(
            collective_id=0, has_side_effects=True, vmem_limit_bytes=63 * 1024 * 1024
        ),
    )(
        chain_first_residue, pairs, gap_embedding, layer_norm_gain,
        layer_norm_bias, output_bias, gate_bias_heads,
        source_alignment_rows, projection_weight, pair_bias_logits, output_weight,
    )


def solution(mesh):
    return jax.shard_map(
        local,
        mesh=mesh,
        in_specs=(
            P("rows", "res", None),
            P(None, "rows"),
            P(),
            P(),
            P(),
            P(),
            P(),
            P(),
            P(None, "res", None),
            P(),
            P(),
        ),
        out_specs=P("rows", "res", None),
        check_vma=False,
    )
```

```python
import functools
import math

import jax
import jax.numpy as jnp
from jax import lax
from jax.experimental import pallas as pl
from jax.experimental.pallas import tpu as pltpu
from jax.sharding import PartitionSpec as P

norm_eps = 1e-05
MESH = pl.DeviceIdType.MESH
f32, bf16, i32 = jnp.float32, jnp.bfloat16, jnp.int32
NT = (((1,), (1,)), ((), ()))
TN = (((0,), (0,)), ((), ()))
CHAIN_PAD = 8


def layer_norm(x, gain, shift):
    center = jnp.mean(x, axis=-1, keepdims=True)
    moved = x - center
    spread = jnp.mean(jnp.square(moved), axis=-1, keepdims=True)
    return moved * lax.rsqrt(spread + norm_eps) * gain + shift


def body(
    R, J, n, cols, heads, chains,
    first_hbm, pairs_hbm, gap_hbm, gain_hbm, shift_hbm, out_shift_hbm, gate_hbm,
    src_hbm, w_hbm, bias_hbm, ow_hbm,
    out_hbm,
    first_ref, pairs_ref, vec_refs,
    src_v, norm_v, w_v, w_wide, wqvg_t, wk_t, ow_v,
    table_v, wanted_v, wanted_s, pos_v, pos_s,
    bias_all, bias_t,
    send_a0, send_a1, recv_a0, recv_a1,
    send_b0, send_b1, recv_b0, recv_b1,
    q_diag, att_v, send_c, gate_col, lifted_v, v_ext, gate_v,
    local_sem, idx_send, idx_recv, bias_send, bias_recv,
    a_send, a_recv, b_send, b0_recv, b1_recv, c_send, c_recv,
):
    L = n * J
    width = 256
    half = width // 2
    N = J * cols
    hd = width // heads
    Y = J // 2
    log2e = math.log2(math.e)
    me_r = lax.axis_index("rows")
    me_j = lax.axis_index("res")
    core = lax.rem(me_j, 2)

    X = 4
    Z = R // X
    me_z, me_x = me_r // X, lax.rem(me_r, X)

    def farthest_first(size, i):
        odd = lax.rem(i, 2)
        return size // 2 + (1 - 2 * odd) * ((i + odd) // 2)

    def row_peer(t):
        z = lax.rem(me_z + farthest_first(Z, lax.rem(t, Z)), Z)
        x = lax.rem(me_x + farthest_first(X, t // Z), X)
        return z * X + x

    def res_peer(t):
        y = lax.rem(me_j // 2 + farthest_first(Y, lax.rem(t, Y)), Y)
        return 2 * y + lax.rem(core + 1 + t // Y, 2)

    load_src = pltpu.make_async_copy(src_hbm, src_v, local_sem.at[0])
    load_w = pltpu.make_async_copy(w_hbm, w_v, local_sem.at[1])
    load_bias = pltpu.make_async_copy(
        bias_hbm, bias_all.at[me_j // 2, core], local_sem.at[2]
    )
    load_ow = pltpu.make_async_copy(ow_hbm, ow_v, local_sem.at[3])
    load_first = pltpu.make_async_copy(first_hbm, first_ref, local_sem.at[6])
    load_pairs = pltpu.make_async_copy(pairs_hbm, pairs_ref, local_sem.at[7])
    load_vecs = [
        pltpu.make_async_copy(v, vec_refs[i], local_sem.at[8 + i])
        for i, v in enumerate([gap_hbm, gain_hbm, shift_hbm, out_shift_hbm, gate_hbm])
    ]
    load_pairs.start()
    load_first.start()
    load_src.start()
    for load in load_vecs:
        load.start()
    load_bias.start()
    load_w.start()
    load_ow.start()

    barrier = pltpu.get_barrier_semaphore()

    @pl.loop(0, R - 1)
    def _(t):
        pl.semaphore_signal(
            barrier, inc=1, device_id={"rows": row_peer(t)}, device_id_type=MESH
        )

    @pl.loop(0, J - 1)
    def _(t):
        pl.semaphore_signal(
            barrier, inc=1, device_id={"res": res_peer(t)}, device_id_type=MESH
        )

    load_pairs.wait()
    listed = pairs_ref[...]
    shift_bits = L.bit_length() - 1
    owner = lax.shift_right_arithmetic(listed, jnp.full_like(listed, shift_bits))
    within = jnp.bitwise_and(listed, L - 1)
    lane = lax.broadcasted_iota(i32, (R, 128), 1)
    row_id = lax.broadcasted_iota(i32, (R, L), 0)
    table = jnp.zeros((R, 128), i32)
    for c in range(chains):
        own_c = owner[c : c + 1, :]
        wit_c = within[c : c + 1, :]
        match = row_id == own_c
        low = jnp.min(jnp.where(match, wit_c, L), axis=1, keepdims=True)
        high = jnp.max(jnp.where(match, wit_c, -1), axis=1, keepdims=True)
        table = jnp.where(lane == c, jnp.minimum(low, L - 1), table)
        table = jnp.where(lane == CHAIN_PAD + c, jnp.maximum(high, 0), table)
        rank = jnp.max(
            jnp.where(match, jnp.where(wit_c > low, 1, 0), 0), axis=0, keepdims=True
        )
        pos_v[c : c + 1, 0:L] = jnp.where(own_c < 0, 2 * R, 2 * own_c + rank)
    table_v[...] = table.reshape(R, 1, 128)
    load_pos = pltpu.make_async_copy(pos_v, pos_s, local_sem.at[4])
    load_pos.start()

    load_first.wait()
    col0 = me_j * cols
    chain_a = jnp.int32(0)
    chain_b = jnp.int32(0)
    for k in range(1, chains):
        chain_a += (first_ref[k] <= col0).astype(i32)
        chain_b += (first_ref[k] <= col0 + cols - 1).astype(i32)
    start_b = first_ref[chain_b] - col0
    in_b = lax.broadcasted_iota(i32, (cols, width), 0) >= start_b
    in_b_half = lax.broadcasted_iota(i32, (cols, half), 0) >= start_b

    pl.semaphore_wait(barrier, R - 1 + J - 1)

    wanted_v[me_r] = table_v[me_r]

    @pl.loop(0, R - 1)
    def _(t):
        b = row_peer(t)
        pltpu.make_async_remote_copy(
            table_v.at[b], wanted_v.at[me_r], idx_send, idx_recv,
            device_id={"rows": b}, device_id_type=MESH,
        ).start()

    load_bias.wait()
    my_bias = bias_all.at[me_j // 2, core]

    @pl.loop(0, Y - 1)
    def _(t):
        pltpu.make_async_remote_copy(
            my_bias, my_bias, bias_send.at[0], bias_recv.at[0],
            device_id={"res": res_peer(Y + t)}, device_id_type=MESH,
        ).start()

    for load in load_vecs:
        load.wait()
    gap, gain, shift, out_shift, gate_shift = [
        v[...].astype(f32).reshape(1, width) for v in vec_refs
    ]
    load_src.wait()
    step = min(16, L)

    @pl.loop(0, L // step)
    def _(i):
        x = src_v[pl.ds(i * step, step)].astype(f32).reshape(step * cols, width)
        y = layer_norm(x, gain, shift).astype(bf16)
        norm_v[pl.ds(i * step, step)] = y.reshape(step, cols, width)

    gap_row = jnp.broadcast_to(layer_norm(gap, gain, shift), (cols, width)).astype(bf16)
    recv_a0[2 * R] = gap_row[:, :half]
    recv_a1[2 * R] = gap_row[:, half:]

    def wait_recv(ref, sem):
        pltpu.make_async_remote_copy(
            ref, ref, idx_send, sem, device_id={"rows": me_r}, device_id_type=MESH
        ).wait_recv()

    def wait_send(ref, sem):
        pltpu.make_async_remote_copy(
            ref, ref, sem, idx_recv, device_id={"rows": me_r}, device_id_type=MESH
        ).wait_send()

    wait_recv(wanted_v.at[pl.ds(0, R - 1)], idx_recv)
    load_wanted = pltpu.make_async_copy(wanted_v, wanted_s, local_sem.at[5])
    load_wanted.start()
    load_wanted.wait()
    load_pos.wait()

    def pick(b, k):
        at_a = jnp.clip(wanted_s[b, 0, k * CHAIN_PAD + chain_a], 0, L - 1)
        at_b = jnp.clip(wanted_s[b, 0, k * CHAIN_PAD + chain_b], 0, L - 1)
        return jnp.where(in_b, norm_v[at_b], norm_v[at_a])

    @pl.loop(0, R - 1)
    def _(t):
        b = row_peer(t)
        for k in range(2):
            cells = pick(b, k)
            send_a0[b, k] = cells[:, :half]
            send_a1[b, k] = cells[:, half:]
        pltpu.make_async_remote_copy(
            send_a0.at[b], recv_a0.at[pl.ds(2 * me_r, 2)], a_send.at[0], a_recv.at[0],
            device_id={"rows": b}, device_id_type=MESH,
        ).start()

    @pl.loop(0, R - 1)
    def _(t):
        b = row_peer(t)
        pltpu.make_async_remote_copy(
            send_a1.at[b], recv_a1.at[pl.ds(2 * me_r, 2)], a_send.at[1], a_recv.at[1],
            device_id={"rows": b}, device_id_type=MESH,
        ).start()

    for k in range(2):
        cells = pick(me_r, k)
        recv_a0[2 * me_r + k] = cells[:, :half]
        recv_a1[2 * me_r + k] = cells[:, half:]

    load_w.wait()
    load_ow.wait()
    w_wide[...] = w_v[...].astype(f32).reshape(width * heads, 128)
    q_diag[...] = jnp.zeros_like(q_diag)
    v_ext[...] = jnp.ones_like(v_ext)

    @pl.loop(0, heads)
    def _(h):
        w_h = w_wide[pl.ds(h, width, stride=heads), :].T.astype(bf16)
        wqvg_t[0, h] = w_h[0:hd]
        wk_t[h] = w_h[hd : 2 * hd]
        wqvg_t[1, h] = w_h[2 * hd : 3 * hd]
        wqvg_t[2, h] = w_h[3 * hd :]

    gate_col[...] = jnp.broadcast_to(gate_shift, (128, width)).T

    wait_recv(recv_a0.at[pl.ds(0, 2 * (R - 1))], a_recv.at[0])

    def regather(recv, s):
        at_a = jnp.clip(pos_s[chain_a, s], 0, 2 * R)
        at_b = jnp.clip(pos_s[chain_b, s], 0, 2 * R)
        return jnp.where(in_b_half, recv[at_b], recv[at_a])

    @pl.loop(0, J - 1)
    def _(t):
        j = res_peer(t)
        for r in range(n):
            send_b0[j, r] = regather(recv_a0, j * n + r)
        pltpu.make_async_remote_copy(
            send_b0.at[j], recv_b0.at[:, me_j], b_send.at[0], b0_recv,
            device_id={"res": j}, device_id_type=MESH,
        ).start()

    for r in range(n):
        recv_b0[r, me_j] = regather(recv_a0, me_j * n + r)

    wait_recv(bias_all.at[pl.ds(0, Y - 1), 0], bias_recv.at[0])
    share = bias_all.at[:, core]
    pltpu.make_async_remote_copy(
        share, share, bias_send.at[1], bias_recv.at[1],
        device_id={"res": me_j + 1 - 2 * core}, device_id_type=MESH,
    ).start()

    wait_recv(bias_all.at[:, 0], bias_recv.at[1])

    @pl.loop(0, heads)
    def _(h):
        block = bias_all[:, :, h].reshape(N, N).astype(f32)
        bias_t[h] = block.T * log2e

    wait_recv(recv_a1.at[pl.ds(0, 2 * (R - 1))], a_recv.at[1])

    @pl.loop(0, n)
    def _(r):
        @pl.loop(0, J - 1, unroll=5)
        def _(t):
            j = res_peer(t)
            send_b1[r, j] = regather(recv_a1, j * n + r)
            pltpu.make_async_remote_copy(
                send_b1.at[r, j], recv_b1.at[r, me_j], b_send.at[1], b1_recv.at[r],
                device_id={"res": j}, device_id_type=MESH,
            ).start()

        recv_b1[r, me_j] = regather(recv_a1, me_j * n + r)

    wait_recv(recv_b0.at[:, pl.ds(0, J - 1)], b0_recv)
    scale = hd ** (-0.5) * log2e

    @pl.loop(0, n)
    def _(r):
        wait_recv(recv_b1.at[r, pl.ds(0, J - 1)], b1_recv.at[r])
        x = jnp.concatenate(
            [recv_b0[r].reshape(N, half), recv_b1[r].reshape(N, half)], axis=1
        )
        qvg = lax.dot_general(
            wqvg_t[...].reshape(3 * width, width), x, NT, preferred_element_type=f32
        )
        keys = lax.dot_general(
            x, wk_t[...].reshape(width, width), NT, preferred_element_type=f32
        ).astype(bf16)
        q = (qvg[:width] * scale).astype(bf16)
        v = qvg[width : 2 * width].astype(bf16)
        gate_v[...] = jax.nn.sigmoid(qvg[2 * width :] + gate_col[:, 0:1])
        for h in range(heads):
            own = slice(h * hd, (h + 1) * hd)
            q_diag[own, h * N : (h + 1) * N] = q[own]
            v_ext[h, :hd, :] = v[own]
        for h in range(heads):
            at = slice(h * N, (h + 1) * N)
            s = jnp.dot(keys, q_diag[:, at], preferred_element_type=f32) + bias_t[h]
            top = jnp.max(s, axis=0, keepdims=True)
            lifted_v[:, at] = jnp.exp2(s - top).astype(bf16)
        for h in range(heads):
            own = slice(h * hd, (h + 1) * hd)
            o = jnp.dot(
                v_ext[h], lifted_v[:, h * N : (h + 1) * N], preferred_element_type=f32
            )
            att_v[own, :] = (o[:hd] * (1.0 / o[hd : hd + 1]) * gate_v[own]).astype(bf16)
        update = lax.dot_general(att_v[...], ow_v[...], TN, preferred_element_type=f32)
        update = (update + out_shift).astype(bf16)
        send_c[pl.ds(r * J, J)] = update.reshape(J, cols, width)

        @pl.loop(0, J - 1)
        def _(t):
            j = res_peer(t)
            pltpu.make_async_remote_copy(
                send_c.at[r * J + j], out_hbm.at[me_j * n + r], c_send, c_recv,
                device_id={"res": j}, device_id_type=MESH,
            ).start()

        pltpu.make_async_copy(
            send_c.at[r * J + me_j], out_hbm.at[me_j * n + r], local_sem.at[13 + r]
        ).start()

    for r in range(n):
        pltpu.make_async_copy(
            send_c.at[r * J + me_j], out_hbm.at[me_j * n + r], local_sem.at[13 + r]
        ).wait()
    wait_send(table_v.at[pl.ds(0, R - 1)], idx_send)
    wait_send(bias_all.at[pl.ds(0, Y - 1), 0], bias_send.at[0])
    wait_send(bias_all.at[:, 0], bias_send.at[1])
    wait_send(send_a0.at[pl.ds(0, R - 1)], a_send.at[0])
    wait_send(send_a1.at[pl.ds(0, R - 1)], a_send.at[1])
    wait_send(send_b0.at[pl.ds(0, J - 1)], b_send.at[0])
    wait_send(send_b1.at[:, pl.ds(0, J - 1)], b_send.at[1])
    wait_send(send_c.at[pl.ds(0, n * (J - 1))], c_send)
    wait_recv(out_hbm.at[pl.ds(0, n * (J - 1))], c_recv)


def local(
    source_alignment_rows,
    pairs,
    chain_first_residue,
    gap_embedding,
    layer_norm_gain,
    layer_norm_bias,
    projection_weight,
    gate_bias_heads,
    pair_bias_logits,
    output_weight,
    output_bias,
):
    R, J = lax.axis_size("rows"), lax.axis_size("res")
    L, cols, width = source_alignment_rows.shape
    heads = projection_weight.shape[1]
    chains = pairs.shape[0]
    n = L // J
    N = J * cols
    half = width // 2
    DMA = pltpu.SemaphoreType.DMA
    hbm = pl.BlockSpec(memory_space=pltpu.HBM)
    return pl.pallas_call(
        functools.partial(body, R, J, n, cols, heads, chains),
        out_shape=jax.ShapeDtypeStruct((L, cols, width), bf16),
        in_specs=[hbm] * 11,
        out_specs=hbm,
        scratch_shapes=[
            pltpu.SMEM((chains,), i32),
            pltpu.VMEM((chains, L), i32),
            [pltpu.VMEM((width,), bf16)] * 5,
            pltpu.VMEM((L, cols, width), bf16),
            pltpu.VMEM((L, cols, width), bf16),
            pltpu.VMEM((width, heads, 128), bf16),
            pltpu.VMEM((width * heads, 128), f32),
            pltpu.VMEM((3, heads, width // heads, width), bf16),
            pltpu.VMEM((heads, width // heads, width), bf16),
            pltpu.VMEM((width, width), bf16),
            pltpu.VMEM((R, 1, 128), i32),
            pltpu.VMEM((R, 1, 128), i32),
            pltpu.SMEM((R, 1, 128), i32),
            pltpu.VMEM((8, 128), i32),
            pltpu.SMEM((8, 128), i32),
            pltpu.VMEM((J // 2, 2, heads, cols, N), bf16),
            pltpu.VMEM((heads, N, N), f32),
            pltpu.VMEM((R, 2, cols, half), bf16),
            pltpu.VMEM((R, 2, cols, half), bf16),
            pltpu.VMEM((2 * R + 1, cols, half), bf16),
            pltpu.VMEM((2 * R + 1, cols, half), bf16),
            pltpu.VMEM((J, n, cols, half), bf16),
            pltpu.VMEM((n, J, cols, half), bf16),
            pltpu.VMEM((n, J, cols, half), bf16),
            pltpu.VMEM((n, J, cols, half), bf16),
            pltpu.VMEM((width, heads * N), bf16),
            pltpu.VMEM((width, N), bf16),
            pltpu.VMEM((n * J, cols, width), bf16),
            pltpu.VMEM((width, 128), f32),
            pltpu.VMEM((N, heads * N), bf16),
            pltpu.VMEM((heads, width // heads + 16, N), bf16),
            pltpu.VMEM((width, N), f32),
            DMA((13 + n,)), DMA, DMA, DMA((2,)), DMA((2,)),
            DMA((2,)), DMA((2,)), DMA((2,)), DMA, DMA((n,)), DMA, DMA,
        ],
        compiler_params=pltpu.CompilerParams(
            collective_id=0, has_side_effects=True, vmem_limit_bytes=63 * 1024 * 1024
        ),
    )(
        chain_first_residue, pairs, gap_embedding, layer_norm_gain,
        layer_norm_bias, output_bias, gate_bias_heads,
        source_alignment_rows, projection_weight, pair_bias_logits, output_weight,
    )


def solution(mesh):
    return jax.shard_map(
        local,
        mesh=mesh,
        in_specs=(
            P("rows", "res", None),
            P(None, "rows"),
            P(),
            P(),
            P(),
            P(),
            P(),
            P(),
            P(None, "res", None),
            P(),
            P(),
        ),
        out_specs=P("rows", "res", None),
        check_vma=False,
    )
```

```python
import functools
import math

import jax
import jax.numpy as jnp
from jax import lax
from jax.experimental import pallas as pl
from jax.experimental.pallas import tpu as pltpu
from jax.sharding import PartitionSpec as P

norm_eps = 1e-05
MESH = pl.DeviceIdType.MESH
f32, bf16, i32 = jnp.float32, jnp.bfloat16, jnp.int32
NT = (((1,), (1,)), ((), ()))
TN = (((0,), (0,)), ((), ()))
CHAIN_PAD = 8


def layer_norm(x, gain, shift):
    center = jnp.mean(x, axis=-1, keepdims=True)
    moved = x - center
    spread = jnp.mean(jnp.square(moved), axis=-1, keepdims=True)
    return moved * lax.rsqrt(spread + norm_eps) * gain + shift


def body(
    R, J, n, cols, heads, chains,
    first_hbm, pairs_hbm, gap_hbm, gain_hbm, shift_hbm, out_shift_hbm, gate_hbm,
    src_hbm, w_hbm, bias_hbm, ow_hbm,
    out_hbm,
    first_ref, pairs_ref, vec_refs,
    src_v, norm_v, w_v, w_wide, wqvg_t, wk_t, ow_v,
    table_v, wanted_v, wanted_s, pos_v, pos_s,
    bias_all, bias_t,
    send_a0, send_a1, recv_a0, recv_a1,
    send_b0, send_b1, recv_b0, recv_b1,
    q_diag, att_v, send_c, gate_col, lifted_v, v_ext, gate_v,
    local_sem, idx_send, idx_recv, bias_send, bias_recv,
    a_send, a_recv, b_send, b0_recv, b1_recv, c_send, c_recv,
):
    L = n * J
    width = 256
    half = width // 2
    N = J * cols
    hd = width // heads
    Y = J // 2
    log2e = math.log2(math.e)
    me_r = lax.axis_index("rows")
    me_j = lax.axis_index("res")
    core = lax.rem(me_j, 2)

    X = 4
    Z = R // X
    me_z, me_x = me_r // X, lax.rem(me_r, X)

    def farthest_first(size, i):
        odd = lax.rem(i, 2)
        return size // 2 + (1 - 2 * odd) * ((i + odd) // 2)

    def row_peer(t):
        z = lax.rem(me_z + farthest_first(Z, lax.rem(t, Z)), Z)
        x = lax.rem(me_x + farthest_first(X, t // Z), X)
        return z * X + x

    def res_peer(t):
        y = lax.rem(me_j // 2 + farthest_first(Y, lax.rem(t, Y)), Y)
        return 2 * y + lax.rem(core + 1 + t // Y, 2)

    load_src = pltpu.make_async_copy(src_hbm, src_v, local_sem.at[0])
    load_w = pltpu.make_async_copy(w_hbm, w_v, local_sem.at[1])
    load_bias = pltpu.make_async_copy(
        bias_hbm, bias_all.at[me_j // 2, core], local_sem.at[2]
    )
    load_ow = pltpu.make_async_copy(ow_hbm, ow_v, local_sem.at[3])
    load_first = pltpu.make_async_copy(first_hbm, first_ref, local_sem.at[6])
    load_pairs = pltpu.make_async_copy(pairs_hbm, pairs_ref, local_sem.at[7])
    load_vecs = [
        pltpu.make_async_copy(v, vec_refs[i], local_sem.at[8 + i])
        for i, v in enumerate([gap_hbm, gain_hbm, shift_hbm, out_shift_hbm, gate_hbm])
    ]
    load_pairs.start()
    load_first.start()
    load_src.start()
    for load in load_vecs:
        load.start()
    load_bias.start()
    load_w.start()
    load_ow.start()

    barrier = pltpu.get_barrier_semaphore()

    @pl.loop(0, R - 1)
    def _(t):
        pl.semaphore_signal(
            barrier, inc=1, device_id={"rows": row_peer(t)}, device_id_type=MESH
        )

    @pl.loop(0, J - 1)
    def _(t):
        pl.semaphore_signal(
            barrier, inc=1, device_id={"res": res_peer(t)}, device_id_type=MESH
        )

    load_pairs.wait()
    listed = pairs_ref[...]
    shift_bits = L.bit_length() - 1
    owner = lax.shift_right_arithmetic(listed, jnp.full_like(listed, shift_bits))
    within = jnp.bitwise_and(listed, L - 1)
    lane = lax.broadcasted_iota(i32, (R, 128), 1)
    row_id = lax.broadcasted_iota(i32, (R, L), 0)
    table = jnp.zeros((R, 128), i32)
    for c in range(chains):
        own_c = owner[c : c + 1, :]
        wit_c = within[c : c + 1, :]
        match = row_id == own_c
        low = jnp.min(jnp.where(match, wit_c, L), axis=1, keepdims=True)
        high = jnp.max(jnp.where(match, wit_c, -1), axis=1, keepdims=True)
        table = jnp.where(lane == c, jnp.minimum(low, L - 1), table)
        table = jnp.where(lane == CHAIN_PAD + c, jnp.maximum(high, 0), table)
        rank = jnp.max(
            jnp.where(match, jnp.where(wit_c > low, 1, 0), 0), axis=0, keepdims=True
        )
        pos_v[c : c + 1, 0:L] = jnp.where(own_c < 0, 2 * R, 2 * own_c + rank)
    table_v[...] = table.reshape(R, 1, 128)
    load_pos = pltpu.make_async_copy(pos_v, pos_s, local_sem.at[4])
    load_pos.start()

    load_first.wait()
    col0 = me_j * cols
    chain_a = jnp.int32(0)
    chain_b = jnp.int32(0)
    for k in range(1, chains):
        chain_a += (first_ref[k] <= col0).astype(i32)
        chain_b += (first_ref[k] <= col0 + cols - 1).astype(i32)
    start_b = first_ref[chain_b] - col0
    in_b = lax.broadcasted_iota(i32, (cols, width), 0) >= start_b
    in_b_half = lax.broadcasted_iota(i32, (cols, half), 0) >= start_b

    pl.semaphore_wait(barrier, R - 1 + J - 1)

    wanted_v[me_r] = table_v[me_r]

    @pl.loop(0, R - 1)
    def _(t):
        b = row_peer(t)
        pltpu.make_async_remote_copy(
            table_v.at[b], wanted_v.at[me_r], idx_send, idx_recv,
            device_id={"rows": b}, device_id_type=MESH,
        ).start()

    load_bias.wait()
    my_bias = bias_all.at[me_j // 2, core]

    @pl.loop(0, Y - 1)
    def _(t):
        pltpu.make_async_remote_copy(
            my_bias, my_bias, bias_send.at[0], bias_recv.at[0],
            device_id={"res": res_peer(Y + t)}, device_id_type=MESH,
        ).start()

    for load in load_vecs:
        load.wait()
    gap, gain, shift, out_shift, gate_shift = [
        v[...].astype(f32).reshape(1, width) for v in vec_refs
    ]
    load_src.wait()
    step = min(8, L)

    @pl.loop(0, L // step)
    def _(i):
        x = src_v[pl.ds(i * step, step)].astype(f32).reshape(step * cols, width)
        y = layer_norm(x, gain, shift).astype(bf16)
        norm_v[pl.ds(i * step, step)] = y.reshape(step, cols, width)

    gap_row = jnp.broadcast_to(layer_norm(gap, gain, shift), (cols, width)).astype(bf16)
    recv_a0[2 * R] = gap_row[:, :half]
    recv_a1[2 * R] = gap_row[:, half:]

    def wait_recv(ref, sem):
        pltpu.make_async_remote_copy(
            ref, ref, idx_send, sem, device_id={"rows": me_r}, device_id_type=MESH
        ).wait_recv()

    def wait_send(ref, sem):
        pltpu.make_async_remote_copy(
            ref, ref, sem, idx_recv, device_id={"rows": me_r}, device_id_type=MESH
        ).wait_send()

    wait_recv(wanted_v.at[pl.ds(0, R - 1)], idx_recv)
    load_wanted = pltpu.make_async_copy(wanted_v, wanted_s, local_sem.at[5])
    load_wanted.start()
    load_wanted.wait()
    load_pos.wait()

    def pick(b, k):
        at_a = jnp.clip(wanted_s[b, 0, k * CHAIN_PAD + chain_a], 0, L - 1)
        at_b = jnp.clip(wanted_s[b, 0, k * CHAIN_PAD + chain_b], 0, L - 1)
        return jnp.where(in_b, norm_v[at_b], norm_v[at_a])

    @pl.loop(0, R - 1)
    def _(t):
        b = row_peer(t)
        for k in range(2):
            cells = pick(b, k)
            send_a0[b, k] = cells[:, :half]
            send_a1[b, k] = cells[:, half:]
        pltpu.make_async_remote_copy(
            send_a0.at[b], recv_a0.at[pl.ds(2 * me_r, 2)], a_send.at[0], a_recv.at[0],
            device_id={"rows": b}, device_id_type=MESH,
        ).start()

    @pl.loop(0, R - 1)
    def _(t):
        b = row_peer(t)
        pltpu.make_async_remote_copy(
            send_a1.at[b], recv_a1.at[pl.ds(2 * me_r, 2)], a_send.at[1], a_recv.at[1],
            device_id={"rows": b}, device_id_type=MESH,
        ).start()

    for k in range(2):
        cells = pick(me_r, k)
        recv_a0[2 * me_r + k] = cells[:, :half]
        recv_a1[2 * me_r + k] = cells[:, half:]

    load_w.wait()
    load_ow.wait()
    w_wide[...] = w_v[...].astype(f32).reshape(width * heads, 128)
    q_diag[...] = jnp.zeros_like(q_diag)
    v_ext[...] = jnp.ones_like(v_ext)

    @pl.loop(0, heads)
    def _(h):
        w_h = w_wide[pl.ds(h, width, stride=heads), :].T.astype(bf16)
        wqvg_t[0, h] = w_h[0:hd]
        wk_t[h] = w_h[hd : 2 * hd]
        wqvg_t[1, h] = w_h[2 * hd : 3 * hd]
        wqvg_t[2, h] = w_h[3 * hd :]

    gate_col[...] = jnp.broadcast_to(gate_shift, (128, width)).T

    wait_recv(recv_a0.at[pl.ds(0, 2 * (R - 1))], a_recv.at[0])

    def regather(recv, s):
        at_a = jnp.clip(pos_s[chain_a, s], 0, 2 * R)
        at_b = jnp.clip(pos_s[chain_b, s], 0, 2 * R)
        return jnp.where(in_b_half, recv[at_b], recv[at_a])

    @pl.loop(0, J - 1)
    def _(t):
        j = res_peer(t)
        for r in range(n):
            send_b0[j, r] = regather(recv_a0, j * n + r)
        pltpu.make_async_remote_copy(
            send_b0.at[j], recv_b0.at[:, me_j], b_send.at[0], b0_recv,
            device_id={"res": j}, device_id_type=MESH,
        ).start()

    for r in range(n):
        recv_b0[r, me_j] = regather(recv_a0, me_j * n + r)

    wait_recv(bias_all.at[pl.ds(0, Y - 1), 0], bias_recv.at[0])
    share = bias_all.at[:, core]
    pltpu.make_async_remote_copy(
        share, share, bias_send.at[1], bias_recv.at[1],
        device_id={"res": me_j + 1 - 2 * core}, device_id_type=MESH,
    ).start()

    wait_recv(bias_all.at[:, 0], bias_recv.at[1])

    @pl.loop(0, heads)
    def _(h):
        block = bias_all[:, :, h].reshape(N, N).astype(f32)
        bias_t[h] = block.T * log2e

    wait_recv(recv_a1.at[pl.ds(0, 2 * (R - 1))], a_recv.at[1])

    @pl.loop(0, n)
    def _(r):
        @pl.loop(0, J - 1)
        def _(t):
            j = res_peer(t)
            send_b1[r, j] = regather(recv_a1, j * n + r)
            pltpu.make_async_remote_copy(
                send_b1.at[r, j], recv_b1.at[r, me_j], b_send.at[1], b1_recv.at[r],
                device_id={"res": j}, device_id_type=MESH,
            ).start()

        recv_b1[r, me_j] = regather(recv_a1, me_j * n + r)

    wait_recv(recv_b0.at[:, pl.ds(0, J - 1)], b0_recv)
    scale = hd ** (-0.5) * log2e

    @pl.loop(0, n)
    def _(r):
        wait_recv(recv_b1.at[r, pl.ds(0, J - 1)], b1_recv.at[r])
        x = jnp.concatenate(
            [recv_b0[r].reshape(N, half), recv_b1[r].reshape(N, half)], axis=1
        )
        qvg = lax.dot_general(
            wqvg_t[...].reshape(3 * width, width), x, NT, preferred_element_type=f32
        )
        keys = lax.dot_general(
            x, wk_t[...].reshape(width, width), NT, preferred_element_type=f32
        ).astype(bf16)
        q = (qvg[:width] * scale).astype(bf16)
        v = qvg[width : 2 * width].astype(bf16)
        gate_v[...] = jax.nn.sigmoid(qvg[2 * width :] + gate_col[:, 0:1])
        for h in range(heads):
            own = slice(h * hd, (h + 1) * hd)
            q_diag[own, h * N : (h + 1) * N] = q[own]
            v_ext[h, :hd, :] = v[own]
        for h in range(heads):
            at = slice(h * N, (h + 1) * N)
            s = jnp.dot(keys, q_diag[:, at], preferred_element_type=f32) + bias_t[h]
            top = jnp.max(s, axis=0, keepdims=True)
            lifted_v[:, at] = jnp.exp2(s - top).astype(bf16)
        for h in range(heads):
            own = slice(h * hd, (h + 1) * hd)
            o = jnp.dot(
                v_ext[h], lifted_v[:, h * N : (h + 1) * N], preferred_element_type=f32
            )
            att_v[own, :] = (o[:hd] * (1.0 / o[hd : hd + 1]) * gate_v[own]).astype(bf16)
        update = lax.dot_general(att_v[...], ow_v[...], TN, preferred_element_type=f32)
        update = (update + out_shift).astype(bf16)
        send_c[pl.ds(r * J, J)] = update.reshape(J, cols, width)

        @pl.loop(0, J - 1)
        def _(t):
            j = res_peer(t)
            pltpu.make_async_remote_copy(
                send_c.at[r * J + j], out_hbm.at[me_j * n + r], c_send, c_recv,
                device_id={"res": j}, device_id_type=MESH,
            ).start()

        pltpu.make_async_copy(
            send_c.at[r * J + me_j], out_hbm.at[me_j * n + r], local_sem.at[13 + r]
        ).start()

    for r in range(n):
        pltpu.make_async_copy(
            send_c.at[r * J + me_j], out_hbm.at[me_j * n + r], local_sem.at[13 + r]
        ).wait()
    wait_send(table_v.at[pl.ds(0, R - 1)], idx_send)
    wait_send(bias_all.at[pl.ds(0, Y - 1), 0], bias_send.at[0])
    wait_send(bias_all.at[:, 0], bias_send.at[1])
    wait_send(send_a0.at[pl.ds(0, R - 1)], a_send.at[0])
    wait_send(send_a1.at[pl.ds(0, R - 1)], a_send.at[1])
    wait_send(send_b0.at[pl.ds(0, J - 1)], b_send.at[0])
    wait_send(send_b1.at[:, pl.ds(0, J - 1)], b_send.at[1])
    wait_send(send_c.at[pl.ds(0, n * (J - 1))], c_send)
    wait_recv(out_hbm.at[pl.ds(0, n * (J - 1))], c_recv)


def local(
    source_alignment_rows,
    pairs,
    chain_first_residue,
    gap_embedding,
    layer_norm_gain,
    layer_norm_bias,
    projection_weight,
    gate_bias_heads,
    pair_bias_logits,
    output_weight,
    output_bias,
):
    R, J = lax.axis_size("rows"), lax.axis_size("res")
    L, cols, width = source_alignment_rows.shape
    heads = projection_weight.shape[1]
    chains = pairs.shape[0]
    n = L // J
    N = J * cols
    half = width // 2
    DMA = pltpu.SemaphoreType.DMA
    hbm = pl.BlockSpec(memory_space=pltpu.HBM)
    return pl.pallas_call(
        functools.partial(body, R, J, n, cols, heads, chains),
        out_shape=jax.ShapeDtypeStruct((L, cols, width), bf16),
        in_specs=[hbm] * 11,
        out_specs=hbm,
        scratch_shapes=[
            pltpu.SMEM((chains,), i32),
            pltpu.VMEM((chains, L), i32),
            [pltpu.VMEM((width,), bf16)] * 5,
            pltpu.VMEM((L, cols, width), bf16),
            pltpu.VMEM((L, cols, width), bf16),
            pltpu.VMEM((width, heads, 128), bf16),
            pltpu.VMEM((width * heads, 128), f32),
            pltpu.VMEM((3, heads, width // heads, width), bf16),
            pltpu.VMEM((heads, width // heads, width), bf16),
            pltpu.VMEM((width, width), bf16),
            pltpu.VMEM((R, 1, 128), i32),
            pltpu.VMEM((R, 1, 128), i32),
            pltpu.SMEM((R, 1, 128), i32),
            pltpu.VMEM((8, 128), i32),
            pltpu.SMEM((8, 128), i32),
            pltpu.VMEM((J // 2, 2, heads, cols, N), bf16),
            pltpu.VMEM((heads, N, N), f32),
            pltpu.VMEM((R, 2, cols, half), bf16),
            pltpu.VMEM((R, 2, cols, half), bf16),
            pltpu.VMEM((2 * R + 1, cols, half), bf16),
            pltpu.VMEM((2 * R + 1, cols, half), bf16),
            pltpu.VMEM((J, n, cols, half), bf16),
            pltpu.VMEM((n, J, cols, half), bf16),
            pltpu.VMEM((n, J, cols, half), bf16),
            pltpu.VMEM((n, J, cols, half), bf16),
            pltpu.VMEM((width, heads * N), bf16),
            pltpu.VMEM((width, N), bf16),
            pltpu.VMEM((n * J, cols, width), bf16),
            pltpu.VMEM((width, 128), f32),
            pltpu.VMEM((N, heads * N), bf16),
            pltpu.VMEM((heads, width // heads + 16, N), bf16),
            pltpu.VMEM((width, N), f32),
            DMA((13 + n,)), DMA, DMA, DMA((2,)), DMA((2,)),
            DMA((2,)), DMA((2,)), DMA((2,)), DMA, DMA((n,)), DMA, DMA,
        ],
        compiler_params=pltpu.CompilerParams(
            collective_id=0, has_side_effects=True, vmem_limit_bytes=63 * 1024 * 1024
        ),
    )(
        chain_first_residue, pairs, gap_embedding, layer_norm_gain,
        layer_norm_bias, output_bias, gate_bias_heads,
        source_alignment_rows, projection_weight, pair_bias_logits, output_weight,
    )


def solution(mesh):
    return jax.shard_map(
        local,
        mesh=mesh,
        in_specs=(
            P("rows", "res", None),
            P(None, "rows"),
            P(),
            P(),
            P(),
            P(),
            P(),
            P(),
            P(None, "res", None),
            P(),
            P(),
        ),
        out_specs=P("rows", "res", None),
        check_vma=False,
    )
```

```python
import functools

import jax
import jax.numpy as jnp
from jax import lax
from jax.experimental import pallas as pl
from jax.experimental.pallas import tpu as pltpu
from jax.sharding import PartitionSpec as P

norm_eps = 1e-05
MESH = pl.DeviceIdType.MESH
f32, bf16, i32 = jnp.float32, jnp.bfloat16, jnp.int32
NT = (((1,), (1,)), ((), ()))
TN = (((0,), (0,)), ((), ()))
CHAIN_PAD = 8


def layer_norm(x, gain, shift):
    center = jnp.mean(x, axis=-1, keepdims=True)
    moved = x - center
    spread = jnp.mean(jnp.square(moved), axis=-1, keepdims=True)
    return moved * lax.rsqrt(spread + norm_eps) * gain + shift


def body(
    R, J, n, cols, heads, chains,
    first_hbm, pairs_hbm, gap_hbm, gain_hbm, shift_hbm, out_shift_hbm, gate_hbm,
    src_hbm, w_hbm, bias_hbm, ow_hbm,
    out_hbm,
    first_ref, pairs_ref, vec_refs,
    src_v, norm_v, w_v, w_wide, wqvg_t, wk_t, ow_v,
    table_v, wanted_v, wanted_s, pos_v, pos_s,
    bias_all, bias_t,
    send_a0, send_a1, recv_a0, recv_a1,
    send_b0, send_b1, recv_b0, recv_b1,
    q_diag, att_v, send_c, gate_col, lifted_v, v_ext, gate_v,
    local_sem, idx_send, idx_recv, bias_send, bias_recv,
    a_send, a_recv, b_send, b0_recv, b1_recv, c_send, c_recv,
):
    L = n * J
    width = 256
    half = width // 2
    N = J * cols
    hd = width // heads
    Y = J // 2
    me_r = lax.axis_index("rows")
    me_j = lax.axis_index("res")
    core = lax.rem(me_j, 2)

    X = 4
    Z = R // X
    me_z, me_x = me_r // X, lax.rem(me_r, X)

    def farthest_first(size, i):
        odd = lax.rem(i, 2)
        return size // 2 + (1 - 2 * odd) * ((i + odd) // 2)

    def row_peer(t):
        z = lax.rem(me_z + farthest_first(Z, lax.rem(t, Z)), Z)
        x = lax.rem(me_x + farthest_first(X, t // Z), X)
        return z * X + x

    def res_peer(t):
        y = lax.rem(me_j // 2 + farthest_first(Y, lax.rem(t, Y)), Y)
        return 2 * y + lax.rem(core + 1 + t // Y, 2)

    load_src = pltpu.make_async_copy(src_hbm, src_v, local_sem.at[0])
    load_w = pltpu.make_async_copy(w_hbm, w_v, local_sem.at[1])
    load_bias = pltpu.make_async_copy(
        bias_hbm, bias_all.at[me_j // 2, core], local_sem.at[2]
    )
    load_ow = pltpu.make_async_copy(ow_hbm, ow_v, local_sem.at[3])
    load_first = pltpu.make_async_copy(first_hbm, first_ref, local_sem.at[6])
    load_pairs = pltpu.make_async_copy(pairs_hbm, pairs_ref, local_sem.at[7])
    load_vecs = [
        pltpu.make_async_copy(v, vec_refs[i], local_sem.at[8 + i])
        for i, v in enumerate([gap_hbm, gain_hbm, shift_hbm, out_shift_hbm, gate_hbm])
    ]
    load_pairs.start()
    load_first.start()
    load_src.start()
    for load in load_vecs:
        load.start()
    load_bias.start()
    load_w.start()
    load_ow.start()

    barrier = pltpu.get_barrier_semaphore()

    @pl.loop(0, R - 1)
    def _(t):
        pl.semaphore_signal(
            barrier, inc=1, device_id={"rows": row_peer(t)}, device_id_type=MESH
        )

    @pl.loop(0, J - 1)
    def _(t):
        pl.semaphore_signal(
            barrier, inc=1, device_id={"res": res_peer(t)}, device_id_type=MESH
        )

    load_pairs.wait()
    listed = pairs_ref[...]
    shift_bits = L.bit_length() - 1
    owner = lax.shift_right_arithmetic(listed, jnp.full_like(listed, shift_bits))
    within = jnp.bitwise_and(listed, L - 1)
    lane = lax.broadcasted_iota(i32, (R, 128), 1)
    row_id = lax.broadcasted_iota(i32, (R, L), 0)
    table = jnp.zeros((R, 128), i32)
    for c in range(chains):
        own_c = owner[c : c + 1, :]
        wit_c = within[c : c + 1, :]
        match = row_id == own_c
        low = jnp.min(jnp.where(match, wit_c, L), axis=1, keepdims=True)
        high = jnp.max(jnp.where(match, wit_c, -1), axis=1, keepdims=True)
        table = jnp.where(lane == c, jnp.minimum(low, L - 1), table)
        table = jnp.where(lane == CHAIN_PAD + c, jnp.maximum(high, 0), table)
        rank = jnp.max(
            jnp.where(match, jnp.where(wit_c > low, 1, 0), 0), axis=0, keepdims=True
        )
        pos_v[c : c + 1, 0:L] = jnp.where(own_c < 0, 2 * R, 2 * own_c + rank)
    table_v[...] = table.reshape(R, 1, 128)
    load_pos = pltpu.make_async_copy(pos_v, pos_s, local_sem.at[4])
    load_pos.start()

    load_first.wait()
    col0 = me_j * cols
    chain_a = jnp.int32(0)
    chain_b = jnp.int32(0)
    for k in range(1, chains):
        chain_a += (first_ref[k] <= col0).astype(i32)
        chain_b += (first_ref[k] <= col0 + cols - 1).astype(i32)
    start_b = first_ref[chain_b] - col0
    in_b = lax.broadcasted_iota(i32, (cols, width), 0) >= start_b
    in_b_half = lax.broadcasted_iota(i32, (cols, half), 0) >= start_b

    pl.semaphore_wait(barrier, R - 1 + J - 1)

    wanted_v[me_r] = table_v[me_r]

    @pl.loop(0, R - 1)
    def _(t):
        b = row_peer(t)
        pltpu.make_async_remote_copy(
            table_v.at[b], wanted_v.at[me_r], idx_send, idx_recv,
            device_id={"rows": b}, device_id_type=MESH,
        ).start()

    load_bias.wait()
    my_bias = bias_all.at[me_j // 2, core]

    @pl.loop(0, Y - 1)
    def _(t):
        pltpu.make_async_remote_copy(
            my_bias, my_bias, bias_send.at[0], bias_recv.at[0],
            device_id={"res": res_peer(Y + t)}, device_id_type=MESH,
        ).start()

    for load in load_vecs:
        load.wait()
    gap, gain, shift, out_shift, gate_shift = [
        v[...].astype(f32).reshape(1, width) for v in vec_refs
    ]
    load_src.wait()
    step = min(8, L)

    @pl.loop(0, L // step)
    def _(i):
        x = src_v[pl.ds(i * step, step)].astype(f32).reshape(step * cols, width)
        y = layer_norm(x, gain, shift).astype(bf16)
        norm_v[pl.ds(i * step, step)] = y.reshape(step, cols, width)

    gap_row = jnp.broadcast_to(layer_norm(gap, gain, shift), (cols, width)).astype(bf16)
    recv_a0[2 * R] = gap_row[:, :half]
    recv_a1[2 * R] = gap_row[:, half:]

    def wait_recv(ref, sem):
        pltpu.make_async_remote_copy(
            ref, ref, idx_send, sem, device_id={"rows": me_r}, device_id_type=MESH
        ).wait_recv()

    def wait_send(ref, sem):
        pltpu.make_async_remote_copy(
            ref, ref, sem, idx_recv, device_id={"rows": me_r}, device_id_type=MESH
        ).wait_send()

    wait_recv(wanted_v.at[pl.ds(0, R - 1)], idx_recv)
    load_wanted = pltpu.make_async_copy(wanted_v, wanted_s, local_sem.at[5])
    load_wanted.start()
    load_wanted.wait()
    load_pos.wait()

    def pick(b, k):
        at_a = jnp.clip(wanted_s[b, 0, k * CHAIN_PAD + chain_a], 0, L - 1)
        at_b = jnp.clip(wanted_s[b, 0, k * CHAIN_PAD + chain_b], 0, L - 1)
        return jnp.where(in_b, norm_v[at_b], norm_v[at_a])

    @pl.loop(0, R - 1)
    def _(t):
        b = row_peer(t)
        for k in range(2):
            cells = pick(b, k)
            send_a0[b, k] = cells[:, :half]
            send_a1[b, k] = cells[:, half:]
        pltpu.make_async_remote_copy(
            send_a0.at[b], recv_a0.at[pl.ds(2 * me_r, 2)], a_send.at[0], a_recv.at[0],
            device_id={"rows": b}, device_id_type=MESH,
        ).start()

    @pl.loop(0, R - 1)
    def _(t):
        b = row_peer(t)
        pltpu.make_async_remote_copy(
            send_a1.at[b], recv_a1.at[pl.ds(2 * me_r, 2)], a_send.at[1], a_recv.at[1],
            device_id={"rows": b}, device_id_type=MESH,
        ).start()

    for k in range(2):
        cells = pick(me_r, k)
        recv_a0[2 * me_r + k] = cells[:, :half]
        recv_a1[2 * me_r + k] = cells[:, half:]

    load_w.wait()
    load_ow.wait()
    w_wide[...] = w_v[...].astype(f32).reshape(width * heads, 128)
    q_diag[...] = jnp.zeros_like(q_diag)
    v_ext[...] = jnp.ones_like(v_ext)

    @pl.loop(0, heads)
    def _(h):
        w_h = w_wide[pl.ds(h, width, stride=heads), :].T.astype(bf16)
        wqvg_t[0, h] = w_h[0:hd]
        wk_t[h] = w_h[hd : 2 * hd]
        wqvg_t[1, h] = w_h[2 * hd : 3 * hd]
        wqvg_t[2, h] = w_h[3 * hd :]

    gate_col[...] = jnp.broadcast_to(gate_shift, (128, width)).T

    wait_recv(recv_a0.at[pl.ds(0, 2 * (R - 1))], a_recv.at[0])

    def regather(recv, s):
        at_a = jnp.clip(pos_s[chain_a, s], 0, 2 * R)
        at_b = jnp.clip(pos_s[chain_b, s], 0, 2 * R)
        return jnp.where(in_b_half, recv[at_b], recv[at_a])

    @pl.loop(0, J - 1)
    def _(t):
        j = res_peer(t)
        for r in range(n):
            send_b0[j, r] = regather(recv_a0, j * n + r)
        pltpu.make_async_remote_copy(
            send_b0.at[j], recv_b0.at[:, me_j], b_send.at[0], b0_recv,
            device_id={"res": j}, device_id_type=MESH,
        ).start()

    for r in range(n):
        recv_b0[r, me_j] = regather(recv_a0, me_j * n + r)

    wait_recv(bias_all.at[pl.ds(0, Y - 1), 0], bias_recv.at[0])
    share = bias_all.at[:, core]
    pltpu.make_async_remote_copy(
        share, share, bias_send.at[1], bias_recv.at[1],
        device_id={"res": me_j + 1 - 2 * core}, device_id_type=MESH,
    ).start()

    wait_recv(bias_all.at[:, 0], bias_recv.at[1])

    @pl.loop(0, heads)
    def _(h):
        block = bias_all[:, :, h].reshape(N, N).astype(f32)
        bias_t[h] = block.T

    wait_recv(recv_a1.at[pl.ds(0, 2 * (R - 1))], a_recv.at[1])

    @pl.loop(0, n)
    def _(r):
        @pl.loop(0, J - 1)
        def _(t):
            j = res_peer(t)
            send_b1[r, j] = regather(recv_a1, j * n + r)
            pltpu.make_async_remote_copy(
                send_b1.at[r, j], recv_b1.at[r, me_j], b_send.at[1], b1_recv.at[r],
                device_id={"res": j}, device_id_type=MESH,
            ).start()

        recv_b1[r, me_j] = regather(recv_a1, me_j * n + r)

    wait_recv(recv_b0.at[:, pl.ds(0, J - 1)], b0_recv)
    scale = hd ** (-0.5)

    @pl.loop(0, n)
    def _(r):
        wait_recv(recv_b1.at[r, pl.ds(0, J - 1)], b1_recv.at[r])
        x = jnp.concatenate(
            [recv_b0[r].reshape(N, half), recv_b1[r].reshape(N, half)], axis=1
        )
        qvg = lax.dot_general(
            wqvg_t[...].reshape(3 * width, width), x, NT, preferred_element_type=f32
        )
        keys = lax.dot_general(
            x, wk_t[...].reshape(width, width), NT, preferred_element_type=f32
        ).astype(bf16)
        q = (qvg[:width] * scale).astype(bf16)
        v = qvg[width : 2 * width].astype(bf16)
        gate_v[...] = jax.nn.sigmoid(qvg[2 * width :] + gate_col[:, 0:1])
        for h in range(heads):
            own = slice(h * hd, (h + 1) * hd)
            q_diag[own, h * N : (h + 1) * N] = q[own]
            v_ext[h, :hd, :] = v[own]
        for h in range(heads):
            at = slice(h * N, (h + 1) * N)
            s = jnp.dot(keys, q_diag[:, at], preferred_element_type=f32) + bias_t[h]
            top = jnp.max(s, axis=0, keepdims=True)
            lifted_v[:, at] = jnp.exp(s - top).astype(bf16)
        for h in range(heads):
            own = slice(h * hd, (h + 1) * hd)
            o = jnp.dot(
                v_ext[h], lifted_v[:, h * N : (h + 1) * N], preferred_element_type=f32
            )
            att_v[own, :] = (o[:hd] * (1.0 / o[hd : hd + 1]) * gate_v[own]).astype(bf16)
        update = lax.dot_general(att_v[...], ow_v[...], TN, preferred_element_type=f32)
        update = (update + out_shift).astype(bf16)
        send_c[pl.ds(r * J, J)] = update.reshape(J, cols, width)

        @pl.loop(0, J - 1)
        def _(t):
            j = res_peer(t)
            pltpu.make_async_remote_copy(
                send_c.at[r * J + j], out_hbm.at[me_j * n + r], c_send, c_recv,
                device_id={"res": j}, device_id_type=MESH,
            ).start()

        pltpu.make_async_copy(
            send_c.at[r * J + me_j], out_hbm.at[me_j * n + r], local_sem.at[13 + r]
        ).start()

    for r in range(n):
        pltpu.make_async_copy(
            send_c.at[r * J + me_j], out_hbm.at[me_j * n + r], local_sem.at[13 + r]
        ).wait()
    wait_send(table_v.at[pl.ds(0, R - 1)], idx_send)
    wait_send(bias_all.at[pl.ds(0, Y - 1), 0], bias_send.at[0])
    wait_send(bias_all.at[:, 0], bias_send.at[1])
    wait_send(send_a0.at[pl.ds(0, R - 1)], a_send.at[0])
    wait_send(send_a1.at[pl.ds(0, R - 1)], a_send.at[1])
    wait_send(send_b0.at[pl.ds(0, J - 1)], b_send.at[0])
    wait_send(send_b1.at[:, pl.ds(0, J - 1)], b_send.at[1])
    wait_send(send_c.at[pl.ds(0, n * (J - 1))], c_send)
    wait_recv(out_hbm.at[pl.ds(0, n * (J - 1))], c_recv)


def local(
    source_alignment_rows,
    pairs,
    chain_first_residue,
    gap_embedding,
    layer_norm_gain,
    layer_norm_bias,
    projection_weight,
    gate_bias_heads,
    pair_bias_logits,
    output_weight,
    output_bias,
):
    R, J = lax.axis_size("rows"), lax.axis_size("res")
    L, cols, width = source_alignment_rows.shape
    heads = projection_weight.shape[1]
    chains = pairs.shape[0]
    n = L // J
    N = J * cols
    half = width // 2
    DMA = pltpu.SemaphoreType.DMA
    hbm = pl.BlockSpec(memory_space=pltpu.HBM)
    return pl.pallas_call(
        functools.partial(body, R, J, n, cols, heads, chains),
        out_shape=jax.ShapeDtypeStruct((L, cols, width), bf16),
        in_specs=[hbm] * 11,
        out_specs=hbm,
        scratch_shapes=[
            pltpu.SMEM((chains,), i32),
            pltpu.VMEM((chains, L), i32),
            [pltpu.VMEM((width,), bf16)] * 5,
            pltpu.VMEM((L, cols, width), bf16),
            pltpu.VMEM((L, cols, width), bf16),
            pltpu.VMEM((width, heads, 128), bf16),
            pltpu.VMEM((width * heads, 128), f32),
            pltpu.VMEM((3, heads, width // heads, width), bf16),
            pltpu.VMEM((heads, width // heads, width), bf16),
            pltpu.VMEM((width, width), bf16),
            pltpu.VMEM((R, 1, 128), i32),
            pltpu.VMEM((R, 1, 128), i32),
            pltpu.SMEM((R, 1, 128), i32),
            pltpu.VMEM((8, 128), i32),
            pltpu.SMEM((8, 128), i32),
            pltpu.VMEM((J // 2, 2, heads, cols, N), bf16),
            pltpu.VMEM((heads, N, N), f32),
            pltpu.VMEM((R, 2, cols, half), bf16),
            pltpu.VMEM((R, 2, cols, half), bf16),
            pltpu.VMEM((2 * R + 1, cols, half), bf16),
            pltpu.VMEM((2 * R + 1, cols, half), bf16),
            pltpu.VMEM((J, n, cols, half), bf16),
            pltpu.VMEM((n, J, cols, half), bf16),
            pltpu.VMEM((n, J, cols, half), bf16),
            pltpu.VMEM((n, J, cols, half), bf16),
            pltpu.VMEM((width, heads * N), bf16),
            pltpu.VMEM((width, N), bf16),
            pltpu.VMEM((n * J, cols, width), bf16),
            pltpu.VMEM((width, 128), f32),
            pltpu.VMEM((N, heads * N), bf16),
            pltpu.VMEM((heads, width // heads + 16, N), bf16),
            pltpu.VMEM((width, N), f32),
            DMA((13 + n,)), DMA, DMA, DMA((2,)), DMA((2,)),
            DMA((2,)), DMA((2,)), DMA((2,)), DMA, DMA((n,)), DMA, DMA,
        ],
        compiler_params=pltpu.CompilerParams(
            collective_id=0, has_side_effects=True, vmem_limit_bytes=63 * 1024 * 1024
        ),
    )(
        chain_first_residue, pairs, gap_embedding, layer_norm_gain,
        layer_norm_bias, output_bias, gate_bias_heads,
        source_alignment_rows, projection_weight, pair_bias_logits, output_weight,
    )


def solution(mesh):
    return jax.shard_map(
        local,
        mesh=mesh,
        in_specs=(
            P("rows", "res", None),
            P(None, "rows"),
            P(),
            P(),
            P(),
            P(),
            P(),
            P(),
            P(None, "res", None),
            P(),
            P(),
        ),
        out_specs=P("rows", "res", None),
        check_vma=False,
    )
```
